128 devices in a mesh: group: 4 (over y), pos: 32 (over x, z, core).
Axes of the slice: x: 4, y: 4, z: 4, core: 2. Of those that a mesh axis runs over, the one named last changes fastest.
Arguments:
- cand_x: bfloat16 [4, 16384, 1024], P('group', 'pos'), may hold values from -6 to 6
- f1_weight: bfloat16 [1024, 4096], replicated, may hold values from -0.1875 to 0.1875
- out_weight: bfloat16 [1024, 1024], replicated, may hold values from -0.1875 to 0.1875
- kv_cache: bfloat16 [4, 4096, 2048], P('group', 'pos'), may hold values from -6 to 6
- user_slot: int32 [4], replicated, may hold values from 0 to 3, each once
- hist_len: int32 [4], replicated, may hold values from 128 to 4096, as said below
- cand_count: int32 [4], replicated, may hold values from 4096 to 16384, as said below
Outputs:
- scored: bfloat16 [4, 16384, 1024], P('group', 'pos')
The draws below stay inside these ranges and needn't reach their ends.
Inputs may be any that keep to these rules, and one draw needn't show every extreme that they name: `hist_len`: lengths are multiples of 128 and some request has the longest history 4096. `cand_count`: some request has all 16384 candidates live. `user_slot`: each cache slot serves exactly one request.
All inputs are finite; a program needn't handle non-finite values.
Results may differ from the reference program's by a relative error of at most 0.0049.
Values may be sent and summed in bfloat16 or wider, within the bound.
A program may use at most 256 MiB of HBM per device.

```python
import math
import jax
import jax.numpy as jnp
from jax import lax

D = 1024
HEADS = 8
REQS = 4
CANDS = 16384
LMAX = 4096


def draw_hist_len(key, part):
    key = jax.random.fold_in(key, 11)
    first, second = jax.random.split(key)
    units = jax.random.randint(first, (REQS,), 1, LMAX // 128 + 1)
    where_max = jax.random.randint(second, (), 0, REQS)
    return (units * 128).at[where_max].set(LMAX).astype(jnp.int32)


def draw_cand_count(key, part):
    key = jax.random.fold_in(key, 23)
    first, second = jax.random.split(key)
    counts = jax.random.randint(first, (REQS,), CANDS // 4, CANDS + 1)
    where_max = jax.random.randint(second, (), 0, REQS)
    return counts.at[where_max].set(CANDS).astype(jnp.int32)


def level_of(rng, dims, cuts, low, high):
    def one(dim, shards_of):
        heights = jax.random.uniform(jax.random.fold_in(jax.random.fold_in(rng, 6), dim), (shards_of,), jnp.float32, low / len(cuts), high / len(cuts))
        return jnp.repeat(jnp.exp(heights), dims[dim] // shards_of).reshape((-1,) + (1,) * (len(dims) - dim - 1))

    gain = one(*cuts[0])
    for cut in cuts[1:]:
        gain = gain * one(*cut)
    return gain


def bell_draw(key, shape, deviation, bound, pieces=(), kind=jnp.bfloat16):
    entries = jax.random.normal(key, shape, jnp.float32) * deviation
    if len(pieces) > 0:
        entries = level_of(key, shape, pieces, -0.22, 0.18) * entries
    return jnp.clip(entries, min=-bound, max=bound).astype(kind)


def setup_inputs(seed: int = 0) -> dict:
    key_of = jax.random.split(jax.random.key(seed), 8)
    return {
        "cand_x": bell_draw(key_of[0], (REQS, CANDS, D), 1.0, 6.0, ((0, 4), (1, 32))),
        "f1_weight": bell_draw(key_of[1], (D, 4 * D), D ** -0.5, 0.1875),
        "out_weight": bell_draw(key_of[2], (D, D), D ** -0.5, 0.1875),
        "kv_cache": bell_draw(key_of[3], (REQS, LMAX, 2 * D), 1.0, 6.0, ((0, 4), (1, 32))),
        "user_slot": jax.random.permutation(key_of[4], REQS).astype(jnp.int32),
        "hist_len": draw_hist_len(jax.random.fold_in(key_of[7], 71), 0),
        "cand_count": draw_cand_count(jax.random.fold_in(key_of[7], 71), 0),
    }


def reference(cand_x, f1_weight, out_weight, kv_cache, user_slot, hist_len, cand_count):
    head_size = D // HEADS
    flat = cand_x.reshape(REQS * CANDS, D)
    proj = jax.nn.silu(jnp.dot(flat, f1_weight, preferred_element_type=jnp.float32)).astype(jnp.bfloat16)
    proj = proj.reshape(REQS, CANDS, 4 * D)

    def one_request(items):
        proj_r, x_r, slot, length, count = items
        gate = proj_r[:, :D]
        own_value = proj_r[:, D:2 * D].reshape(CANDS, HEADS, head_size).astype(jnp.float32)
        query = proj_r[:, 2 * D:3 * D].reshape(CANDS, HEADS, head_size).astype(jnp.float32)
        own_key = proj_r[:, 3 * D:].reshape(CANDS, HEADS, head_size).astype(jnp.float32)
        history = lax.dynamic_index_in_dim(kv_cache, slot, 0, keepdims=False)
        keys = history[:, :D].reshape(LMAX, HEADS, head_size).astype(jnp.float32)
        values = history[:, D:].reshape(LMAX, HEADS, head_size).astype(jnp.float32)
        denom = (length + 1).astype(jnp.float32)
        live = jnp.arange(LMAX, dtype=jnp.int32) < length

        def one_head(parts):
            query_h, keys_h, values_h = parts
            scores = jnp.einsum('cd,ld->cl', query_h, keys_h) / math.sqrt(head_size)
            weights = jnp.where(live[None, :], jax.nn.silu(scores) / denom, 0.0).astype(jnp.bfloat16)
            return jnp.einsum('cl,ld->cd', weights.astype(jnp.float32), values_h)
        attn = lax.map(one_head, (query.transpose(1, 0, 2), keys.transpose(1, 0, 2), values.transpose(1, 0, 2)))
        attn = attn.transpose(1, 0, 2)
        self_score = lax.optimization_barrier(jnp.sum(query * own_key, axis=-1)) / math.sqrt(head_size)
        self_weight = (jax.nn.silu(self_score) / denom).astype(jnp.bfloat16)
        attn = attn + self_weight.astype(jnp.float32)[:, :, None] * own_value
        attn = attn.reshape(CANDS, D)
        mean = lax.optimization_barrier(jnp.mean(attn, axis=-1, keepdims=True))
        centered = attn - mean
        var = lax.optimization_barrier(jnp.mean(centered * centered, axis=-1, keepdims=True))
        normed = centered * lax.rsqrt(var + 1e-05)
        mixed = (normed * gate.astype(jnp.float32)).astype(jnp.bfloat16)
        result = x_r.astype(jnp.float32) + jnp.dot(mixed, out_weight, preferred_element_type=jnp.float32)
        live_c = jnp.arange(CANDS, dtype=jnp.int32) < count
        return jnp.where(live_c[:, None], result, 0.0).astype(jnp.bfloat16)
    return lax.map(one_request, (proj, cand_x, user_slot, hist_len, cand_count))
```

```python
import math

import jax
import jax.numpy as jnp
from jax import lax
from jax.experimental import pallas as pl
from jax.experimental.pallas import tpu as pltpu
from jax.sharding import PartitionSpec as P

MESH = pl.DeviceIdType.MESH
HEADS = 8
HD = 128
D = 1024
ROWS = 512
HIST = 128
NQ = 4
R = HIST // NQ
PART = 32 * R
COLS = 256


def silu(v):
    h = 0.5 * v
    return h + h * jnp.tanh(h)


def wait_bytes(ref, sem):
    pltpu.make_async_copy(ref, ref, sem).wait()


def kernel(
    slot_ref, len_ref, count_ref, x_hbm, f1_hbm, ow_hbm, kv_hbm, out_ref,
    xv, f1v, owv, kvin, st1, st2, kvbuf, projv, qbuf, acc, asend, abuf, selfv,
    load_sem, f1_sem, s1s, s1r, s2s, s2r, xs, xr, qs, qr, os, orr,
):
    y = lax.axis_index("group")
    pos = lax.axis_index("pos")
    c = lax.rem(pos, 2)
    z = lax.rem(pos // 2, 4)
    x = pos // 8
    line = z * 2 + c

    def at(xx, zz, cc):
        return (xx * 4 + zz) * 2 + cc

    kv_loads = [
        pltpu.make_async_copy(kv_hbm.at[:, pl.ds(i * D, D)], kvin.at[i], load_sem.at[i]) for i in range(2)
    ]
    for cp in kv_loads:
        cp.start()
    x_load = pltpu.make_async_copy(x_hbm, xv, load_sem.at[2])
    x_load.start()
    f1_loads = {}
    for i in (2, 3, 1, 0):
        cols = pl.ds(i * D, D)
        f1_loads[i] = pltpu.make_async_copy(f1_hbm.at[:, cols], f1v.at[:, cols], f1_sem.at[i])
        f1_loads[i].start()
    ow_load = pltpu.make_async_copy(ow_hbm, owv, load_sem.at[3])
    ow_load.start()

    barrier = pltpu.get_barrier_semaphore()

    def greet(g, p):
        pl.semaphore_signal(barrier, inc=1, device_id=(g, p), device_id_type=MESH)

    for d in range(1, 4):
        greet(lax.rem(y + d, 4), pos)
        greet(y, at(lax.rem(x + d, 4), z, c))
    for dz in range(4):
        for dc in range(2):
            if dz or dc:
                greet(y, at(x, lax.rem(z + dz, 4), lax.rem(c + dc, 2)))
    for yy in range(4):
        for dc in range(2):
            who = (yy, at(x, lax.rem(z + 4 - yy, 4), lax.rem(c + dc, 2)))
            if yy == 0 and dc == 0:
                @pl.when(y != 0)
                def _():
                    greet(*who)
            else:
                greet(*who)

    @pl.when(y == 0)
    def _():
        pl.semaphore_wait(barrier, 20)

    @pl.when(y != 0)
    def _():
        pl.semaphore_wait(barrier, 21)

    for cp in kv_loads:
        cp.wait()

    def pair_cols(yy):
        return pl.ds(pl.multiple_of(lax.rem(z + yy, 4) * 256, 256), 256)

    for q in range(NQ):
        rows = pl.ds(q * R, R)
        for d in (2, 1, 3):
            yy = lax.rem(y + d, 4)
            pltpu.make_async_remote_copy(
                src_ref=kvin.at[:, rows, pair_cols(yy)],
                dst_ref=st1[q].at[y],
                send_sem=s1s,
                recv_sem=s1r.at[q],
                device_id=(yy, pos),
                device_id_type=MESH,
            ).start()
        st1[q][y] = kvin[:, rows, pair_cols(y)]

    def project(i):
        f1_loads[i].wait()

        def tile(n, carry):
            cols = pl.ds(pl.multiple_of(i * D + n * COLS, COLS), COLS)
            v = jnp.dot(xv[...], f1v[:, cols], preferred_element_type=jnp.float32)
            projv[:, cols] = silu(v).astype(jnp.bfloat16)
            return carry

        lax.fori_loop(0, D // COLS, tile, 0)

    x_load.wait()
    project(2)

    def head_cols(base, head):
        return pl.ds(pl.multiple_of(base * D + head * HD, HD), HD)

    for dz in (2, 1, 3, 0):
        for dc in range(2):
            if dz or dc:
                zz, cc = lax.rem(z + dz, 4), lax.rem(c + dc, 2)
                pltpu.make_async_remote_copy(
                    src_ref=projv.at[:, head_cols(2, zz * 2 + cc)],
                    dst_ref=qbuf.at[line],
                    send_sem=qs,
                    recv_sem=qr,
                    device_id=(y, at(x, zz, cc)),
                    device_id_type=MESH,
                ).start()
    qbuf[line] = projv[:, head_cols(2, line)]

    def stage2(q):
        rows = pl.ds(q * R, R)
        wait_bytes(st1[q].at[pl.ds(0, 3)], s1r.at[q])
        for r in range(4):
            s = slot_ref[r]
            live = (pos * HIST < len_ref[r]).astype(jnp.bfloat16)
            both = st1[q][s]
            for cc in range(2):
                st2[r, cc, 0, rows, :] = both[0, :, cc * HD : (cc + 1) * HD]
                st2[r, cc, 1, rows, :] = both[1, :, cc * HD : (cc + 1) * HD] * live
        zz = lax.rem(z + y, 4)
        for d in (2, 1, 3, 0):
            r = lax.rem(y + d, 4)
            for dc in range(2):
                cc = lax.rem(c + dc, 2)
                src = st2.at[r, cc, :, rows, :]
                dst = kvbuf.at[:, q, x, line]

                def remote():
                    pltpu.make_async_remote_copy(
                        src_ref=src,
                        dst_ref=dst,
                        send_sem=s2s,
                        recv_sem=s2r.at[q],
                        device_id=(r, at(x, zz, cc)),
                        device_id_type=MESH,
                    ).start()

                if d == 0 and dc == 0:
                    pl.when(y != 0)(remote)

                    @pl.when(y == 0)
                    def _():
                        pltpu.make_async_copy(src, dst, s2r.at[q]).start()
                else:
                    remote()

    def share(q):
        wait_bytes(kvbuf.at[:, q, x], s2r.at[q])
        for d in (2, 1, 3):
            pltpu.make_async_remote_copy(
                src_ref=kvbuf.at[:, q, x],
                dst_ref=kvbuf.at[:, q, x],
                send_sem=xs,
                recv_sem=xr.at[q],
                device_id=(y, at(lax.rem(x + d, 4), z, c)),
                device_id_type=MESH,
            ).start()

    denom = (len_ref[y] + 1).astype(jnp.float32)
    scale = 1.0 / math.sqrt(HD)

    def own_term():
        def tile(n, carry):
            rows = pl.ds(pl.multiple_of(n * 128, 128), 128)
            for h in range(HEADS):
                lo = h * HD
                qh = projv[rows, 2 * D + lo : 2 * D + lo + HD].astype(jnp.float32)
                kh = projv[rows, 3 * D + lo : 3 * D + lo + HD].astype(jnp.float32)
                vh = projv[rows, D + lo : D + lo + HD].astype(jnp.float32)
                score = jnp.sum(qh * kh, axis=-1, keepdims=True) * scale
                weight = (silu(score) / denom).astype(jnp.bfloat16).astype(jnp.float32)
                selfv[rows, lo : lo + HD] = weight * vh
            return carry

        lax.fori_loop(0, ROWS // 128, tile, 0)

    stage2(0)
    project(3)
    stage2(1)
    share(0)
    project(1)
    stage2(2)
    share(1)
    project(0)
    stage2(3)
    share(2)
    own_term()
    share(3)

    wait_bytes(qbuf.at[pl.ds(0, 7)], qr)

    def attend(q, qv):
        k = kvbuf[0, q].reshape(PART, HD)
        v = kvbuf[1, q].reshape(PART, HD)
        s = lax.dot_general(qv, k, (((1,), (1,)), ((), ())), preferred_element_type=jnp.float32)
        w = silu(s * scale).astype(jnp.bfloat16)
        return jnp.dot(w, v, preferred_element_type=jnp.float32)

    for q in range(NQ - 1):
        wait_bytes(kvbuf.at[:, q, pl.ds(0, 3)], xr.at[q])

        def block(b, carry, q=q):
            part = pl.ds(b * 2, 2)
            o = attend(q, qbuf[part].reshape(2 * ROWS, HD)).reshape(2, ROWS, HD)
            if q == 0:
                acc[part] = o
            else:
                acc[part] += o
            return carry

        lax.fori_loop(0, 4, block, 0)

    wait_bytes(kvbuf.at[:, NQ - 1, pl.ds(0, 3)], xr.at[NQ - 1])

    def last(i, carry):
        zz = lax.rem(z + i // 2 + 1, 4)
        cc = lax.rem(c + i + 1, 2)
        b = zz * 2 + cc
        o = acc[b] + attend(NQ - 1, qbuf[b])
        asend[b] = (o / denom).astype(jnp.bfloat16)

        @pl.when(i < 7)
        def _():
            pltpu.make_async_remote_copy(
                src_ref=asend.at[b],
                dst_ref=abuf.at[line],
                send_sem=os,
                recv_sem=orr,
                device_id=(y, at(x, zz, cc)),
                device_id_type=MESH,
            ).start()

        return carry

    lax.fori_loop(0, 8, last, 0)
    abuf[line] = asend[line]

    ow_load.wait()
    wait_bytes(abuf.at[pl.ds(0, 7)], orr)
    count = count_ref[y]

    def finish(n, carry):
        rows = pl.ds(pl.multiple_of(n * 128, 128), 128)
        attn = jnp.concatenate([abuf[h, rows, :] for h in range(HEADS)], axis=-1).astype(jnp.float32)
        attn = attn + selfv[rows, :]
        mean = jnp.mean(attn, axis=-1, keepdims=True)
        centered = attn - mean
        var = jnp.mean(centered * centered, axis=-1, keepdims=True)
        normed = centered * lax.rsqrt(var + 1e-05)
        mixed = (normed * projv[rows, 0:D].astype(jnp.float32)).astype(jnp.bfloat16)
        result = xv[rows, :].astype(jnp.float32) + jnp.dot(mixed, owv[...], preferred_element_type=jnp.float32)
        ids = pos * ROWS + n * 128 + lax.broadcasted_iota(jnp.int32, (128, 1), 0)
        out_ref[rows, :] = jnp.where(ids < count, result, 0.0).astype(jnp.bfloat16)
        return carry

    lax.fori_loop(0, ROWS // 128, finish, 0)

    for q in range(NQ):
        wait_bytes(st1[q].at[pl.ds(0, 3)], s1s)
    wait_bytes(qbuf.at[pl.ds(0, 7)], qs)

    @pl.when(y == 0)
    def _():
        wait_bytes(st2.at[pl.ds(0, 3)], s2s)
        wait_bytes(st2.at[0, 0], s2s)

    @pl.when(y != 0)
    def _():
        wait_bytes(st2, s2s)

    wait_bytes(kvbuf.at[:, :, pl.ds(0, 3)], xs)
    wait_bytes(abuf.at[pl.ds(0, 7)], os)


def body(cand_x, f1_weight, out_weight, kv_cache, user_slot, hist_len, cand_count):
    bf = jnp.bfloat16
    smem = pl.BlockSpec(memory_space=pltpu.SMEM)
    hbm = pl.BlockSpec(memory_space=pl.ANY)
    dma = pltpu.SemaphoreType.DMA
    out = pl.pallas_call(
        kernel,
        out_shape=jax.ShapeDtypeStruct((ROWS, D), bf),
        in_specs=[smem] * 3 + [hbm] * 4,
        out_specs=pl.BlockSpec(memory_space=pltpu.VMEM),
        scratch_shapes=[
            pltpu.VMEM((ROWS, D), bf),
            pltpu.VMEM((D, 4 * D), bf),
            pltpu.VMEM((D, D), bf),
            pltpu.VMEM((2, HIST, D), bf),
            [pltpu.VMEM((4, 2, R, 2 * HD), bf)] * NQ,
            pltpu.VMEM((4, 2, 2, HIST, HD), bf),
            pltpu.VMEM((2, NQ, 4, 8, R, HD), bf),
            pltpu.VMEM((ROWS, 4 * D), bf),
            pltpu.VMEM((8, ROWS, HD), bf),
            pltpu.VMEM((8, ROWS, HD), jnp.float32),
            pltpu.VMEM((8, ROWS, HD), bf),
            pltpu.VMEM((8, ROWS, HD), bf),
            pltpu.VMEM((ROWS, D), jnp.float32),
            dma((4,)),
            dma((4,)),
            dma,
            dma((NQ,)),
            dma,
            dma((NQ,)),
            dma,
            dma((NQ,)),
            dma,
            dma,
            dma,
            dma,
        ],
        compiler_params=pltpu.CompilerParams(
            collective_id=0, has_side_effects=True, vmem_limit_bytes=60 * 2**20
        ),
    )(
        user_slot, hist_len, cand_count,
        cand_x.reshape(ROWS, D), f1_weight, out_weight, kv_cache.reshape(HIST, 2 * D),
    )
    return out.reshape(1, ROWS, D)


def solution(mesh):
    placed = (P("group", "pos", None), P(), P(), P("group", "pos", None), P(), P(), P())
    return jax.shard_map(
        body, mesh=mesh, in_specs=placed, out_specs=P("group", "pos", None), check_vma=False
    )
```

```python
import math

import jax
import jax.numpy as jnp
from jax import lax
from jax.experimental import pallas as pl
from jax.experimental.pallas import tpu as pltpu
from jax.sharding import PartitionSpec as P

MESH = pl.DeviceIdType.MESH
HEADS = 8
HD = 128
D = 1024
ROWS = 512
HIST = 128
NQ = 4
R = HIST // NQ
PART = 32 * R
COLS = 256


def silu(v):
    h = 0.5 * v
    return h + h * jnp.tanh(h)


def wait_bytes(ref, sem):
    pltpu.make_async_copy(ref, ref, sem).wait()


def kernel(
    slot_ref, len_ref, count_ref, x_hbm, f1_hbm, ow_hbm, kv_hbm, out_ref,
    xv, f1v, owv, kvin, st1, st2, kvbuf, projv, qbuf, acc, asend, abuf, selfv,
    load_sem, f1_sem, s1s, s1r, s2s, s2r, xs, xr, qs, qr, os, orr,
):
    y = lax.axis_index("group")
    pos = lax.axis_index("pos")
    c = lax.rem(pos, 2)
    z = lax.rem(pos // 2, 4)
    x = pos // 8
    chip = x * 4 + z

    def at(xx, zz, cc):
        return (xx * 4 + zz) * 2 + cc

    def head_at(xx, zz):
        a = lax.rem(xx + 4 - zz, 4)
        return (lax.rem(a, 2) * 2 + lax.rem(xx, 2)) * 2 + a // 2

    mine = head_at(x, z)
    offsets = [
        (1 + 2 * c, 1 + 2 * c), (1 + 2 * c, 3 - 2 * c), (2 - 2 * c, 2 * c),
        (1, 0), (3, 0), (0, 1), (0, 3), (0, 0),
    ]

    kv_loads = [
        pltpu.make_async_copy(kv_hbm.at[:, pl.ds(i * D, D)], kvin.at[i], load_sem.at[i]) for i in range(2)
    ]
    for cp in kv_loads:
        cp.start()
    x_load = pltpu.make_async_copy(x_hbm, xv, load_sem.at[2])
    x_load.start()
    f1_loads = {}
    for i in (2, 3, 1, 0):
        cols = pl.ds(i * D, D)
        f1_loads[i] = pltpu.make_async_copy(f1_hbm.at[:, cols], f1v.at[:, cols], f1_sem.at[i])
        f1_loads[i].start()
    ow_load = pltpu.make_async_copy(ow_hbm, owv, load_sem.at[3])
    ow_load.start()

    barrier = pltpu.get_barrier_semaphore()

    def greet(g, p):
        pl.semaphore_signal(barrier, inc=1, device_id=(g, p), device_id_type=MESH)

    for d in range(1, 4):
        greet(lax.rem(y + d, 4), pos)
    greet(y, at(x, z, 1 - c))
    for dx, dz in offsets[:7]:
        greet(y, at(lax.rem(x + 4 - dx, 4), lax.rem(z + 4 - dz, 4), c))
        greet(y, at(lax.rem(x + dx, 4), lax.rem(z + dz, 4), c))
    for yy in range(4):
        for m in range(2):
            for n in range(2):
                dx, dz = yy % 2 + 2 * m, yy // 2 + 2 * n
                who = (yy, at(lax.rem(x + 4 - dx, 4), lax.rem(z + 4 - dz, 4), c))
                if yy == 0 and m == 0 and n == 0:
                    @pl.when(y != 0)
                    def _():
                        greet(*who)
                else:
                    greet(*who)

    @pl.when(y == 0)
    def _():
        pl.semaphore_wait(barrier, 33)

    @pl.when(y != 0)
    def _():
        pl.semaphore_wait(barrier, 34)

    for cp in kv_loads:
        cp.wait()

    def pair_cols(yy):
        odd = lax.rem(yy, 2)
        pair = lax.rem(x + z + odd + yy // 2, 2) * 2 + lax.rem(x + odd, 2)
        return pl.ds(pl.multiple_of(pair * 256, 256), 256)

    for q in range(NQ):
        rows = pl.ds(q * R, R)
        for d in (2, 1, 3):
            yy = lax.rem(y + d, 4)
            pltpu.make_async_remote_copy(
                src_ref=kvin.at[:, rows, pair_cols(yy)],
                dst_ref=st1[q].at[y],
                send_sem=s1s,
                recv_sem=s1r.at[q],
                device_id=(yy, pos),
                device_id_type=MESH,
            ).start()
        st1[q][y] = kvin[:, rows, pair_cols(y)]

    def project(i):
        f1_loads[i].wait()

        def tile(n, carry):
            cols = pl.ds(pl.multiple_of(i * D + n * COLS, COLS), COLS)
            v = jnp.dot(xv[...], f1v[:, cols], preferred_element_type=jnp.float32)
            projv[:, cols] = silu(v).astype(jnp.bfloat16)
            return carry

        lax.fori_loop(0, D // COLS, tile, 0)

    x_load.wait()
    project(2)

    def head_cols(base, head):
        return pl.ds(pl.multiple_of(base * D + head * HD, HD), HD)

    for k in range(7):
        xx, zz = lax.rem(x + offsets[k][0], 4), lax.rem(z + offsets[k][1], 4)
        pltpu.make_async_remote_copy(
            src_ref=projv.at[:, head_cols(2, head_at(xx, zz))],
            dst_ref=qbuf.at[k],
            send_sem=qs,
            recv_sem=qr,
            device_id=(y, at(xx, zz, c)),
            device_id_type=MESH,
        ).start()
    qbuf[7] = projv[:, head_cols(2, mine)]

    def stage2(q):
        rows = pl.ds(q * R, R)
        wait_bytes(st1[q].at[pl.ds(0, 3)], s1r.at[q])
        for r in range(4):
            s = slot_ref[r]
            live = (pos * HIST < len_ref[r]).astype(jnp.bfloat16)
            both = st1[q][s]
            for cc in range(2):
                st2[r, cc, 0, rows, :] = both[0, :, cc * HD : (cc + 1) * HD]
                st2[r, cc, 1, rows, :] = both[1, :, cc * HD : (cc + 1) * HD] * live
        for d in (2, 1, 3, 0):
            r = lax.rem(y + d, 4)
            for m in (1, 0):
                for n in (1, 0):
                    xx = lax.rem(x + lax.rem(y, 2) + 2 * m, 4)
                    zz = lax.rem(z + y // 2 + 2 * n, 4)
                    j = lax.rem(xx + 4 - zz, 4) // 2
                    src = st2.at[r, j, :, rows, :]
                    dst = kvbuf.at[:, q, c, chip]

                    def remote():
                        pltpu.make_async_remote_copy(
                            src_ref=src,
                            dst_ref=dst,
                            send_sem=s2s,
                            recv_sem=s2r.at[q],
                            device_id=(r, at(xx, zz, c)),
                            device_id_type=MESH,
                        ).start()

                    if d == 0 and m == 0 and n == 0:
                        pl.when(y != 0)(remote)

                        @pl.when(y == 0)
                        def _():
                            pltpu.make_async_copy(src, dst, s2r.at[q]).start()
                    else:
                        remote()

    def share(q):
        wait_bytes(kvbuf.at[:, q, c], s2r.at[q])
        pltpu.make_async_remote_copy(
            src_ref=kvbuf.at[:, q, c],
            dst_ref=kvbuf.at[:, q, c],
            send_sem=xs,
            recv_sem=xr.at[q],
            device_id=(y, at(x, z, 1 - c)),
            device_id_type=MESH,
        ).start()

    denom = (len_ref[y] + 1).astype(jnp.float32)
    scale = 1.0 / math.sqrt(HD)

    def own_term():
        def tile(n, carry):
            rows = pl.ds(pl.multiple_of(n * 128, 128), 128)
            for h in range(HEADS):
                lo = h * HD
                qh = projv[rows, 2 * D + lo : 2 * D + lo + HD].astype(jnp.float32)
                kh = projv[rows, 3 * D + lo : 3 * D + lo + HD].astype(jnp.float32)
                vh = projv[rows, D + lo : D + lo + HD].astype(jnp.float32)
                score = jnp.sum(qh * kh, axis=-1, keepdims=True) * scale
                weight = (silu(score) / denom).astype(jnp.bfloat16).astype(jnp.float32)
                selfv[rows, lo : lo + HD] = weight * vh
            return carry

        lax.fori_loop(0, ROWS // 128, tile, 0)

    stage2(0)
    project(3)
    stage2(1)
    share(0)
    project(1)
    stage2(2)
    share(1)
    project(0)
    stage2(3)
    share(2)
    own_term()
    share(3)

    wait_bytes(qbuf.at[pl.ds(0, 7)], qr)

    def attend(q, qv):
        k = kvbuf[0, q].reshape(PART, HD)
        v = kvbuf[1, q].reshape(PART, HD)
        s = lax.dot_general(qv, k, (((1,), (1,)), ((), ())), preferred_element_type=jnp.float32)
        w = silu(s * scale).astype(jnp.bfloat16)
        return jnp.dot(w, v, preferred_element_type=jnp.float32)

    for q in range(NQ - 1):
        wait_bytes(kvbuf.at[:, q, 1 - c], xr.at[q])

        def block(b, carry, q=q):
            part = pl.ds(b * 2, 2)
            o = attend(q, qbuf[part].reshape(2 * ROWS, HD)).reshape(2, ROWS, HD)
            if q == 0:
                acc[part] = o
            else:
                acc[part] += o
            return carry

        lax.fori_loop(0, 4, block, 0)

    wait_bytes(kvbuf.at[:, NQ - 1, 1 - c], xr.at[NQ - 1])

    for k in range(8):
        o = (acc[k] + attend(NQ - 1, qbuf[k])) / denom
        if k == 7:
            abuf[mine] = o.astype(jnp.bfloat16)
        else:
            asend[k] = o.astype(jnp.bfloat16)
            pltpu.make_async_remote_copy(
                src_ref=asend.at[k],
                dst_ref=abuf.at[mine],
                send_sem=os,
                recv_sem=orr,
                device_id=(y, at(lax.rem(x + 4 - offsets[k][0], 4), lax.rem(z + 4 - offsets[k][1], 4), c)),
                device_id_type=MESH,
            ).start()

    ow_load.wait()
    wait_bytes(abuf.at[pl.ds(0, 7)], orr)
    count = count_ref[y]

    def finish(n, carry):
        rows = pl.ds(pl.multiple_of(n * 128, 128), 128)
        attn = jnp.concatenate([abuf[h, rows, :] for h in range(HEADS)], axis=-1).astype(jnp.float32)
        attn = attn + selfv[rows, :]
        mean = jnp.mean(attn, axis=-1, keepdims=True)
        centered = attn - mean
        var = jnp.mean(centered * centered, axis=-1, keepdims=True)
        normed = centered * lax.rsqrt(var + 1e-05)
        mixed = (normed * projv[rows, 0:D].astype(jnp.float32)).astype(jnp.bfloat16)
        result = xv[rows, :].astype(jnp.float32) + jnp.dot(mixed, owv[...], preferred_element_type=jnp.float32)
        ids = pos * ROWS + n * 128 + lax.broadcasted_iota(jnp.int32, (128, 1), 0)
        out_ref[rows, :] = jnp.where(ids < count, result, 0.0).astype(jnp.bfloat16)
        return carry

    lax.fori_loop(0, ROWS // 128, finish, 0)

    for q in range(NQ):
        wait_bytes(st1[q].at[pl.ds(0, 3)], s1s)
    wait_bytes(qbuf.at[pl.ds(0, 7)], qs)

    @pl.when(y == 0)
    def _():
        wait_bytes(st2.at[pl.ds(0, 3)], s2s)
        wait_bytes(st2.at[pl.ds(0, 3)], s2s)
        wait_bytes(st2.at[0, 0], s2s)
        wait_bytes(st2.at[0, 0], s2s)
        wait_bytes(st2.at[0, 0], s2s)

    @pl.when(y != 0)
    def _():
        wait_bytes(st2, s2s)
        wait_bytes(st2, s2s)

    wait_bytes(kvbuf.at[:, :, 0], xs)
    wait_bytes(abuf.at[pl.ds(0, 7)], os)


def body(cand_x, f1_weight, out_weight, kv_cache, user_slot, hist_len, cand_count):
    bf = jnp.bfloat16
    smem = pl.BlockSpec(memory_space=pltpu.SMEM)
    hbm = pl.BlockSpec(memory_space=pl.ANY)
    dma = pltpu.SemaphoreType.DMA
    out = pl.pallas_call(
        kernel,
        out_shape=jax.ShapeDtypeStruct((ROWS, D), bf),
        in_specs=[smem] * 3 + [hbm] * 4,
        out_specs=pl.BlockSpec(memory_space=pltpu.VMEM),
        scratch_shapes=[
            pltpu.VMEM((ROWS, D), bf),
            pltpu.VMEM((D, 4 * D), bf),
            pltpu.VMEM((D, D), bf),
            pltpu.VMEM((2, HIST, D), bf),
            [pltpu.VMEM((4, 2, R, 2 * HD), bf)] * NQ,
            pltpu.VMEM((4, 2, 2, HIST, HD), bf),
            pltpu.VMEM((2, NQ, 2, 16, R, HD), bf),
            pltpu.VMEM((ROWS, 4 * D), bf),
            pltpu.VMEM((8, ROWS, HD), bf),
            pltpu.VMEM((8, ROWS, HD), jnp.float32),
            pltpu.VMEM((7, ROWS, HD), bf),
            pltpu.VMEM((8, ROWS, HD), bf),
            pltpu.VMEM((ROWS, D), jnp.float32),
            dma((4,)),
            dma((4,)),
            dma,
            dma((NQ,)),
            dma,
            dma((NQ,)),
            dma,
            dma((NQ,)),
            dma,
            dma,
            dma,
            dma,
        ],
        compiler_params=pltpu.CompilerParams(
            collective_id=0, has_side_effects=True, vmem_limit_bytes=60 * 2**20
        ),
    )(
        user_slot, hist_len, cand_count,
        cand_x.reshape(ROWS, D), f1_weight, out_weight, kv_cache.reshape(HIST, 2 * D),
    )
    return out.reshape(1, ROWS, D)


def solution(mesh):
    placed = (P("group", "pos", None), P(), P(), P("group", "pos", None), P(), P(), P())
    return jax.shard_map(
        body, mesh=mesh, in_specs=placed, out_specs=P("group", "pos", None), check_vma=False
    )
```

```python
import math

import jax
import jax.numpy as jnp
from jax import lax
from jax.experimental import pallas as pl
from jax.experimental.pallas import tpu as pltpu
from jax.sharding import PartitionSpec as P

MESH = pl.DeviceIdType.MESH
HEADS = 8
HD = 128
D = 1024
ROWS = 512
HIST = 128
NQ = 4
R = HIST // NQ
SPANS = ((0, 1), (1, 2), (2, 4))
NS = len(SPANS)
LAST = NS - 1
WIDE = [(b - a) * R for a, b in SPANS]
COLS = 256
SPREAD = (10, 2, 8, 6, 14, 9, 11, 5, 7, 13, 15, 1, 3, 4, 12, 0)


def silu(v):
    h = 0.5 * v
    return h + h * jnp.tanh(h)


def wait_bytes(ref, sem):
    pltpu.make_async_copy(ref, ref, sem).wait()


def kernel(
    slot_ref, len_ref, count_ref, x_hbm, f1_hbm, ow_hbm, kv_hbm, out_ref,
    xv, f1v, owv, kvin, st1, st2, sel, kvbuf, projv, qbuf, acc, asend, abuf, selfv,
    load_sem, f1_sem, s1s, s1r, s2s, s2r, s3s, s3r, xs, xr, qs, qr, os, orr,
    in_plane,
):
    y = lax.axis_index("group")
    pos = lax.axis_index("pos")
    c = lax.rem(pos, 2)
    z = lax.rem(pos // 2, 4)
    x = pos // 8
    chip = x * 4 + z

    def at(xx, zz, cc):
        return (xx * 4 + zz) * 2 + cc

    def head_at(xx, zz):
        a = lax.rem(xx + 4 - zz, 4)
        return (lax.rem(a, 2) * 2 + lax.rem(xx, 2)) * 2 + a // 2

    mine = head_at(x, z)
    offsets = [
        (1 + 2 * c, 1 + 2 * c), (1 + 2 * c, 3 - 2 * c), (2 - 2 * c, 2 * c),
        (1, 0), (3, 0), (0, 1), (0, 3), (0, 0),
    ]

    kv_loads = [
        pltpu.make_async_copy(kv_hbm.at[:, pl.ds(i * D, D)], kvin.at[i], load_sem.at[i]) for i in range(2)
    ]
    for cp in kv_loads:
        cp.start()
    x_load = pltpu.make_async_copy(x_hbm, xv, load_sem.at[2])
    x_load.start()
    f1_loads = {}
    for i in (2, 3, 1, 0):
        cols = pl.ds(i * D, D)
        f1_loads[i] = pltpu.make_async_copy(f1_hbm.at[:, cols], f1v.at[:, cols], f1_sem.at[i])
        f1_loads[i].start()
    ow_load = pltpu.make_async_copy(ow_hbm, owv, load_sem.at[3])
    ow_load.start()

    barrier = pltpu.get_barrier_semaphore()

    def greet(sem, g, p):
        pl.semaphore_signal(sem, inc=1, device_id=(g, p), device_id_type=MESH)

    def greet_x(sem):
        for d in range(1, 4):
            greet(sem, y, at(lax.rem(x + d, 4), z, c))

    def greet_y(sem):
        for d in range(1, 4):
            greet(sem, lax.rem(y + d, 4), pos)

    greet_y(barrier)
    greet_x(barrier)
    for d in range(1, 4):
        greet(barrier, y, at(x, lax.rem(z + d, 4), c))
    greet(barrier, y, at(x, z, 1 - c))
    pl.semaphore_wait(barrier, 10)

    for cp in kv_loads:
        cp.wait()

    def pair_cols(yy):
        return pl.ds(pl.multiple_of(yy * 256, 256), 256)

    for q in range(NQ):
        rows = pl.ds(q * R, R)
        for d in (2, 1, 3):
            yy = lax.rem(y + d, 4)
            pltpu.make_async_remote_copy(
                src_ref=kvin.at[:, rows, pair_cols(yy)],
                dst_ref=st1[q].at[y],
                send_sem=s1s,
                recv_sem=s1r.at[q],
                device_id=(yy, pos),
                device_id_type=MESH,
            ).start()
        st1[q][y] = kvin[:, rows, pair_cols(y)]

    greet_x(in_plane)
    pl.semaphore_wait(in_plane, 3)

    def project(i):
        f1_loads[i].wait()

        def tile(n, carry):
            cols = pl.ds(pl.multiple_of(i * D + n * COLS, COLS), COLS)
            v = jnp.dot(xv[...], f1v[:, cols], preferred_element_type=jnp.float32)
            projv[:, cols] = silu(v).astype(jnp.bfloat16)
            return carry

        lax.fori_loop(0, D // COLS, tile, 0)

    x_load.wait()
    project(2)

    def head_cols(base, head):
        return pl.ds(pl.multiple_of(base * D + head * HD, HD), HD)

    for k in range(7):
        xx, zz = lax.rem(x + offsets[k][0], 4), lax.rem(z + offsets[k][1], 4)
        pltpu.make_async_remote_copy(
            src_ref=projv.at[:, head_cols(2, head_at(xx, zz))],
            dst_ref=qbuf.at[k],
            send_sem=qs,
            recv_sem=qr,
            device_id=(y, at(xx, zz, c)),
            device_id_type=MESH,
        ).start()
    qbuf[7] = projv[:, head_cols(2, mine)]

    def stage2(q):
        wait_bytes(st1[q].at[pl.ds(0, 3)], s1r.at[q])
        g = [i for i in range(NS) if SPANS[i][0] <= q < SPANS[i][1]][0]
        rows = pl.ds((q - SPANS[g][0]) * R, R)
        for r in range(4):
            s = slot_ref[r]
            live = (pos * HIST < len_ref[r]).astype(jnp.bfloat16)
            both = st1[q][s]
            for j in range(2):
                st2[r, q, j, 0] = both[0, :, j * HD : (j + 1) * HD]
                st2[r, q, j, 1] = both[1, :, j * HD : (j + 1) * HD] * live
        for d in (2, 1, 3):
            r = lax.rem(y + d, 4)
            pltpu.make_async_remote_copy(
                src_ref=st2.at[r, q],
                dst_ref=sel[g].at[y, :, :, rows, :],
                send_sem=s2s,
                recv_sem=s2r.at[q],
                device_id=(r, pos),
                device_id_type=MESH,
            ).start()
        sel[g][y, :, :, rows, :] = st2[y, q]

    def stage3(g):
        for q in range(*SPANS[g]):
            wait_bytes(st2.at[pl.ds(0, 3), q], s2r.at[q])
        for d in SPREAD:
            xx, zz = lax.rem(x + d // 4, 4), lax.rem(z + d % 4, 4)
            h = head_at(xx, zz)
            src = sel[g].at[h // 2, lax.rem(h, 2)]
            dst = kvbuf[g].at[:, c, chip]
            if d == 0:
                pltpu.make_async_copy(src, dst, s3r.at[g]).start()
            else:
                pltpu.make_async_remote_copy(
                    src_ref=src,
                    dst_ref=dst,
                    send_sem=s3s,
                    recv_sem=s3r.at[g],
                    device_id=(y, at(xx, zz, c)),
                    device_id_type=MESH,
                ).start()

    def share(g):
        wait_bytes(kvbuf[g].at[:, c], s3r.at[g])
        pltpu.make_async_remote_copy(
            src_ref=kvbuf[g].at[:, c],
            dst_ref=kvbuf[g].at[:, c],
            send_sem=xs,
            recv_sem=xr.at[g],
            device_id=(y, at(x, z, 1 - c)),
            device_id_type=MESH,
        ).start()

    denom = (len_ref[y] + 1).astype(jnp.float32)
    scale = 1.0 / math.sqrt(HD)

    def own_term():
        def tile(n, carry):
            rows = pl.ds(pl.multiple_of(n * 128, 128), 128)
            for h in range(HEADS):
                lo = h * HD
                qh = projv[rows, 2 * D + lo : 2 * D + lo + HD].astype(jnp.float32)
                kh = projv[rows, 3 * D + lo : 3 * D + lo + HD].astype(jnp.float32)
                vh = projv[rows, D + lo : D + lo + HD].astype(jnp.float32)
                score = jnp.sum(qh * kh, axis=-1, keepdims=True) * scale
                weight = (silu(score) / denom).astype(jnp.bfloat16).astype(jnp.float32)
                selfv[rows, lo : lo + HD] = weight * vh
            return carry

        lax.fori_loop(0, ROWS // 128, tile, 0)

    pieces = [lambda: project(3), lambda: project(1), lambda: project(0), own_term]
    ready = [b for a, b in SPANS]
    stage2(0)
    done = 0
    for q in range(1, NQ):
        stage2(q)
        for piece in pieces[(q - 1) * 4 // (NQ - 1) : q * 4 // (NQ - 1)]:
            piece()
        if ready[done] <= q:
            stage3(done)
            done += 1
    while done < NS:
        stage3(done)
        done += 1

    def attend(g, half, qv):
        k = kvbuf[g][0, half].reshape(16 * WIDE[g], HD)
        v = kvbuf[g][1, half].reshape(16 * WIDE[g], HD)
        s = lax.dot_general(qv, k, (((1,), (1,)), ((), ())), preferred_element_type=jnp.float32)
        w = silu(s * scale).astype(jnp.bfloat16)
        return jnp.dot(w, v, preferred_element_type=jnp.float32)

    def attend_all(g, half, first):
        count = 8 if WIDE[g] == R else 4

        def block(b, carry):
            part = pl.ds(b * count, count)
            o = attend(g, half, qbuf[part].reshape(count * ROWS, HD)).reshape(count, ROWS, HD)
            if first:
                acc[part] = o
            else:
                acc[part] += o
            return carry

        lax.fori_loop(0, 8 // count, block, 0)

    for g in range(LAST):
        share(g)
        if g == 0:
            wait_bytes(qbuf.at[pl.ds(0, 7)], qr)
        attend_all(g, c, g == 0)
        wait_bytes(kvbuf[g].at[:, 1 - c], xr.at[g])
        attend_all(g, 1 - c, False)

    share(LAST)
    wait_bytes(kvbuf[LAST].at[:, 1 - c], xr.at[LAST])
    steps_x = sum(v * 4**i for i, v in enumerate((1, 1, 2, 1, 3, 0, 0, 0)))
    steps_x = steps_x + c * (sum(v * 4**i for i, v in enumerate((3, 3, 0, 1, 3, 0, 0, 0))) - steps_x)
    steps_z = sum(v * 4**i for i, v in enumerate((1, 3, 0, 0, 0, 1, 3, 0)))
    steps_z = steps_z + c * (sum(v * 4**i for i, v in enumerate((3, 1, 2, 0, 0, 1, 3, 0))) - steps_z)

    def last(k, place):
        qv = qbuf[k]
        o = (acc[k] + attend(LAST, 0, qv) + attend(LAST, 1, qv)) / denom
        asend[k] = o.astype(jnp.bfloat16)
        xx = lax.rem(x + 4 - lax.rem(steps_x // place, 4), 4)
        zz = lax.rem(z + 4 - lax.rem(steps_z // place, 4), 4)

        @pl.when(k < 7)
        def _():
            pltpu.make_async_remote_copy(
                src_ref=asend.at[k],
                dst_ref=abuf.at[mine],
                send_sem=os,
                recv_sem=orr,
                device_id=(y, at(xx, zz, c)),
                device_id_type=MESH,
            ).start()

        return place * 4

    lax.fori_loop(0, 8, last, 1)
    abuf[mine] = asend[7]

    ow_load.wait()
    wait_bytes(abuf.at[pl.ds(0, 7)], orr)
    count = count_ref[y]

    def finish(n, carry):
        rows = pl.ds(pl.multiple_of(n * 128, 128), 128)
        attn = jnp.concatenate([abuf[h, rows, :] for h in range(HEADS)], axis=-1).astype(jnp.float32)
        attn = attn + selfv[rows, :]
        mean = jnp.mean(attn, axis=-1, keepdims=True)
        centered = attn - mean
        var = jnp.mean(centered * centered, axis=-1, keepdims=True)
        normed = centered * lax.rsqrt(var + 1e-05)
        mixed = (normed * projv[rows, 0:D].astype(jnp.float32)).astype(jnp.bfloat16)
        result = xv[rows, :].astype(jnp.float32) + jnp.dot(mixed, owv[...], preferred_element_type=jnp.float32)
        ids = pos * ROWS + n * 128 + lax.broadcasted_iota(jnp.int32, (128, 1), 0)
        out_ref[rows, :] = jnp.where(ids < count, result, 0.0).astype(jnp.bfloat16)
        return carry

    lax.fori_loop(0, ROWS // 128, finish, 0)

    for q in range(NQ):
        wait_bytes(st1[q].at[pl.ds(0, 3)], s1s)
    wait_bytes(qbuf.at[pl.ds(0, 7)], qs)

    wait_bytes(st2.at[pl.ds(0, 3)], s2s)
    for g in range(NS):
        wait_bytes(kvbuf[g].at[:, 0, pl.ds(0, 15)], s3s)
        wait_bytes(kvbuf[g].at[:, 0], xs)
    wait_bytes(abuf.at[pl.ds(0, 7)], os)


def body(cand_x, f1_weight, out_weight, kv_cache, user_slot, hist_len, cand_count):
    bf = jnp.bfloat16
    smem = pl.BlockSpec(memory_space=pltpu.SMEM)
    hbm = pl.BlockSpec(memory_space=pl.ANY)
    dma = pltpu.SemaphoreType.DMA
    out = pl.pallas_call(
        kernel,
        out_shape=jax.ShapeDtypeStruct((ROWS, D), bf),
        in_specs=[smem] * 3 + [hbm] * 4,
        out_specs=pl.BlockSpec(memory_space=pltpu.VMEM),
        scratch_shapes=[
            pltpu.VMEM((ROWS, D), bf),
            pltpu.VMEM((D, 4 * D), bf),
            pltpu.VMEM((D, D), bf),
            pltpu.VMEM((2, HIST, D), bf),
            [pltpu.VMEM((4, 2, R, 2 * HD), bf)] * NQ,
            pltpu.VMEM((4, NQ, 2, 2, R, HD), bf),
            [pltpu.VMEM((4, 2, 2, w, HD), bf) for w in WIDE],
            [pltpu.VMEM((2, 2, 16, w, HD), bf) for w in WIDE],
            pltpu.VMEM((ROWS, 4 * D), bf),
            pltpu.VMEM((8, ROWS, HD), bf),
            pltpu.VMEM((8, ROWS, HD), jnp.float32),
            pltpu.VMEM((8, ROWS, HD), bf),
            pltpu.VMEM((8, ROWS, HD), bf),
            pltpu.VMEM((ROWS, D), jnp.float32),
            dma((4,)),
            dma((4,)),
            dma,
            dma((NQ,)),
            dma,
            dma((NQ,)),
            dma,
            dma((NS,)),
            dma,
            dma((NS,)),
            dma,
            dma,
            dma,
            dma,
            pltpu.SemaphoreType.REGULAR,
        ],
        compiler_params=pltpu.CompilerParams(
            collective_id=0, has_side_effects=True, vmem_limit_bytes=60 * 2**20
        ),
    )(
        user_slot, hist_len, cand_count,
        cand_x.reshape(ROWS, D), f1_weight, out_weight, kv_cache.reshape(HIST, 2 * D),
    )
    return out.reshape(1, ROWS, D)


def solution(mesh):
    placed = (P("group", "pos", None), P(), P(), P("group", "pos", None), P(), P(), P())
    return jax.shard_map(
        body, mesh=mesh, in_specs=placed, out_specs=P("group", "pos", None), check_vma=False
    )
```

```python
import math

import jax
import jax.numpy as jnp
from jax import lax
from jax.experimental import pallas as pl
from jax.experimental.pallas import tpu as pltpu
from jax.sharding import PartitionSpec as P

MESH = pl.DeviceIdType.MESH
HEADS = 8
HD = 128
D = 1024
ROWS = 512
HIST = 128
NQ = 4
R = HIST // NQ
SPANS = ((0, 1), (1, 2), (2, 4))
NS = len(SPANS)
LAST = NS - 1
WIDE = [(b - a) * R for a, b in SPANS]
COLS = 256
SPREAD = (10, 2, 8, 6, 14, 9, 11, 5, 7, 13, 15, 1, 3, 4, 12, 0)


def silu(v):
    h = 0.5 * v
    return h + h * jnp.tanh(h)


def wait_bytes(ref, sem):
    pltpu.make_async_copy(ref, ref, sem).wait()


def kernel(
    slot_ref, len_ref, x_hbm, f1_hbm, ow_hbm, kv_hbm, out_ref,
    xv, f1v, owv, kvin, st1, st2, sel, kvbuf, projv, qbuf, acc, asend, abuf, selfv,
    load_sem, f1_sem, s1s, s1r, s2s, s2r, s3s, s3r, xs, xr, qs, qr, os, orr,
    in_plane,
):
    y = lax.axis_index("group")
    pos = lax.axis_index("pos")
    c = lax.rem(pos, 2)
    z = lax.rem(pos // 2, 4)
    x = pos // 8
    chip = x * 4 + z

    def at(xx, zz, cc):
        return (xx * 4 + zz) * 2 + cc

    def head_at(xx, zz):
        a = lax.rem(xx + 4 - zz, 4)
        return (lax.rem(a, 2) * 2 + lax.rem(xx, 2)) * 2 + a // 2

    mine = head_at(x, z)
    offsets = [
        (1 + 2 * c, 1 + 2 * c), (1 + 2 * c, 3 - 2 * c), (2 - 2 * c, 2 * c),
        (1, 0), (3, 0), (0, 1), (0, 3), (0, 0),
    ]

    kv_loads = [
        pltpu.make_async_copy(kv_hbm.at[:, pl.ds(i * D, D)], kvin.at[i], load_sem.at[i]) for i in range(2)
    ]
    for cp in kv_loads:
        cp.start()
    x_load = pltpu.make_async_copy(x_hbm, xv, load_sem.at[2])
    x_load.start()
    f1_loads = {}
    for i in (2, 3, 1, 0):
        cols = pl.ds(i * D, D)
        f1_loads[i] = pltpu.make_async_copy(f1_hbm.at[:, cols], f1v.at[:, cols], f1_sem.at[i])
        f1_loads[i].start()
    ow_load = pltpu.make_async_copy(ow_hbm, owv, load_sem.at[3])
    ow_load.start()

    barrier = pltpu.get_barrier_semaphore()

    def greet(sem, g, p):
        pl.semaphore_signal(sem, inc=1, device_id=(g, p), device_id_type=MESH)

    def greet_x(sem):
        for d in range(1, 4):
            greet(sem, y, at(lax.rem(x + d, 4), z, c))

    def greet_y(sem):
        for d in range(1, 4):
            greet(sem, lax.rem(y + d, 4), pos)

    greet_y(barrier)
    greet_x(barrier)
    for d in range(1, 4):
        greet(barrier, y, at(x, lax.rem(z + d, 4), c))
    greet(barrier, y, at(x, z, 1 - c))
    pl.semaphore_wait(barrier, 10)

    for cp in kv_loads:
        cp.wait()

    def pair_cols(yy):
        return pl.ds(pl.multiple_of(yy * 256, 256), 256)

    for q in range(NQ):
        rows = pl.ds(q * R, R)
        for d in (2, 1, 3):
            yy = lax.rem(y + d, 4)
            pltpu.make_async_remote_copy(
                src_ref=kvin.at[:, rows, pair_cols(yy)],
                dst_ref=st1[q].at[y],
                send_sem=s1s,
                recv_sem=s1r.at[q],
                device_id=(yy, pos),
                device_id_type=MESH,
            ).start()
        st1[q][y] = kvin[:, rows, pair_cols(y)]

    greet_x(in_plane)
    pl.semaphore_wait(in_plane, 3)

    def project(i):
        f1_loads[i].wait()

        def tile(n, carry):
            cols = pl.ds(pl.multiple_of(i * D + n * COLS, COLS), COLS)
            v = jnp.dot(xv[...], f1v[:, cols], preferred_element_type=jnp.float32)
            projv[:, cols] = silu(v).astype(jnp.bfloat16)
            return carry

        lax.fori_loop(0, D // COLS, tile, 0)

    x_load.wait()
    project(2)

    def head_cols(base, head):
        return pl.ds(pl.multiple_of(base * D + head * HD, HD), HD)

    for k in range(7):
        xx, zz = lax.rem(x + offsets[k][0], 4), lax.rem(z + offsets[k][1], 4)
        pltpu.make_async_remote_copy(
            src_ref=projv.at[:, head_cols(2, head_at(xx, zz))],
            dst_ref=qbuf.at[k],
            send_sem=qs,
            recv_sem=qr,
            device_id=(y, at(xx, zz, c)),
            device_id_type=MESH,
        ).start()
    qbuf[7] = projv[:, head_cols(2, mine)]

    def stage2(q):
        wait_bytes(st1[q].at[pl.ds(0, 3)], s1r.at[q])
        g = [i for i in range(NS) if SPANS[i][0] <= q < SPANS[i][1]][0]
        rows = pl.ds((q - SPANS[g][0]) * R, R)
        for r in range(4):
            s = slot_ref[r]
            live = (pos * HIST < len_ref[r]).astype(jnp.bfloat16)
            both = st1[q][s]
            for j in range(2):
                st2[r, q, j, 0] = both[0, :, j * HD : (j + 1) * HD]
                st2[r, q, j, 1] = both[1, :, j * HD : (j + 1) * HD] * live
        for d in (2, 1, 3):
            r = lax.rem(y + d, 4)
            pltpu.make_async_remote_copy(
                src_ref=st2.at[r, q],
                dst_ref=sel[g].at[y, :, :, rows, :],
                send_sem=s2s,
                recv_sem=s2r.at[q],
                device_id=(r, pos),
                device_id_type=MESH,
            ).start()
        sel[g][y, :, :, rows, :] = st2[y, q]

    def stage3(g):
        for q in range(*SPANS[g]):
            wait_bytes(st2.at[pl.ds(0, 3), q], s2r.at[q])
        for d in SPREAD:
            xx, zz = lax.rem(x + d // 4, 4), lax.rem(z + d % 4, 4)
            h = head_at(xx, zz)
            src = sel[g].at[h // 2, lax.rem(h, 2)]
            dst = kvbuf[g].at[:, c, chip]
            if d == 0:
                pltpu.make_async_copy(src, dst, s3r.at[g]).start()
            else:
                pltpu.make_async_remote_copy(
                    src_ref=src,
                    dst_ref=dst,
                    send_sem=s3s,
                    recv_sem=s3r.at[g],
                    device_id=(y, at(xx, zz, c)),
                    device_id_type=MESH,
                ).start()

    def share(g):
        wait_bytes(kvbuf[g].at[:, c], s3r.at[g])
        pltpu.make_async_remote_copy(
            src_ref=kvbuf[g].at[:, c],
            dst_ref=kvbuf[g].at[:, c],
            send_sem=xs,
            recv_sem=xr.at[g],
            device_id=(y, at(x, z, 1 - c)),
            device_id_type=MESH,
        ).start()

    denom = (len_ref[y] + 1).astype(jnp.float32)
    scale = 1.0 / math.sqrt(HD)

    def own_term():
        def tile(n, carry):
            rows = pl.ds(pl.multiple_of(n * 128, 128), 128)
            for h in range(HEADS):
                lo = h * HD
                qh = projv[rows, 2 * D + lo : 2 * D + lo + HD].astype(jnp.float32)
                kh = projv[rows, 3 * D + lo : 3 * D + lo + HD].astype(jnp.float32)
                vh = projv[rows, D + lo : D + lo + HD].astype(jnp.float32)
                score = jnp.sum(qh * kh, axis=-1, keepdims=True) * scale
                weight = (silu(score) / denom).astype(jnp.bfloat16).astype(jnp.float32)
                selfv[rows, lo : lo + HD] = weight * vh
            return carry

        lax.fori_loop(0, ROWS // 128, tile, 0)

    stage2(0)
    stage2(1)
    project(3)
    project(1)
    stage2(2)
    project(0)
    stage3(0)
    stage2(3)
    own_term()
    stage3(1)
    stage3(2)

    def attend(g, half, qv):
        k = kvbuf[g][0, half].reshape(16 * WIDE[g], HD)
        v = kvbuf[g][1, half].reshape(16 * WIDE[g], HD)
        s = lax.dot_general(qv, k, (((1,), (1,)), ((), ())), preferred_element_type=jnp.float32)
        w = silu(s * scale).astype(jnp.bfloat16)
        return jnp.dot(w, v, preferred_element_type=jnp.float32)

    def attend_all(g, half, first):
        count = 8 if WIDE[g] == R else 4

        def block(b, carry):
            part = pl.ds(b * count, count)
            o = attend(g, half, qbuf[part].reshape(count * ROWS, HD)).reshape(count, ROWS, HD)
            if first:
                acc[part] = o
            else:
                acc[part] += o
            return carry

        lax.fori_loop(0, 8 // count, block, 0)

    for g in range(LAST):
        share(g)
        if g == 0:
            wait_bytes(qbuf.at[pl.ds(0, 7)], qr)
        attend_all(g, c, g == 0)
        wait_bytes(kvbuf[g].at[:, 1 - c], xr.at[g])
        attend_all(g, 1 - c, False)

    share(LAST)
    wait_bytes(kvbuf[LAST].at[:, 1 - c], xr.at[LAST])
    steps_x = sum(v * 4**i for i, v in enumerate((1, 1, 2, 1, 3, 0, 0, 0)))
    steps_x = steps_x + c * (sum(v * 4**i for i, v in enumerate((3, 3, 0, 1, 3, 0, 0, 0))) - steps_x)
    steps_z = sum(v * 4**i for i, v in enumerate((1, 3, 0, 0, 0, 1, 3, 0)))
    steps_z = steps_z + c * (sum(v * 4**i for i, v in enumerate((3, 1, 2, 0, 0, 1, 3, 0))) - steps_z)

    def last(k, place):
        qv = qbuf[k]
        o = (acc[k] + attend(LAST, 0, qv) + attend(LAST, 1, qv)) / denom
        asend[k] = o.astype(jnp.bfloat16)
        xx = lax.rem(x + 4 - lax.rem(steps_x // place, 4), 4)
        zz = lax.rem(z + 4 - lax.rem(steps_z // place, 4), 4)

        @pl.when(k < 7)
        def _():
            pltpu.make_async_remote_copy(
                src_ref=asend.at[k],
                dst_ref=abuf.at[mine],
                send_sem=os,
                recv_sem=orr,
                device_id=(y, at(xx, zz, c)),
                device_id_type=MESH,
            ).start()

        return place * 4

    lax.fori_loop(0, 8, last, 1)
    abuf[mine] = asend[7]

    ow_load.wait()
    wait_bytes(abuf.at[pl.ds(0, 7)], orr)

    def finish(n, carry):
        rows = pl.ds(pl.multiple_of(n * 128, 128), 128)
        attn = jnp.concatenate([abuf[h, rows, :] for h in range(HEADS)], axis=-1).astype(jnp.float32)
        attn = attn + selfv[rows, :]
        mean = jnp.mean(attn, axis=-1, keepdims=True)
        centered = attn - mean
        var = jnp.mean(centered * centered, axis=-1, keepdims=True)
        normed = centered * lax.rsqrt(var + 1e-05)
        mixed = (normed * projv[rows, 0:D].astype(jnp.float32)).astype(jnp.bfloat16)
        result = xv[rows, :].astype(jnp.float32) + jnp.dot(mixed, owv[...], preferred_element_type=jnp.float32)
        out_ref[rows, :] = result.astype(jnp.bfloat16)
        return carry

    lax.fori_loop(0, ROWS // 128, finish, 0)

    for q in range(NQ):
        wait_bytes(st1[q].at[pl.ds(0, 3)], s1s)
    wait_bytes(qbuf.at[pl.ds(0, 7)], qs)

    wait_bytes(st2.at[pl.ds(0, 3)], s2s)
    for g in range(NS):
        wait_bytes(kvbuf[g].at[:, 0, pl.ds(0, 15)], s3s)
        wait_bytes(kvbuf[g].at[:, 0], xs)
    wait_bytes(abuf.at[pl.ds(0, 7)], os)


def body(cand_x, f1_weight, out_weight, kv_cache, user_slot, hist_len, cand_count):
    bf = jnp.bfloat16
    smem = pl.BlockSpec(memory_space=pltpu.SMEM)
    hbm = pl.BlockSpec(memory_space=pl.ANY)
    dma = pltpu.SemaphoreType.DMA
    out = pl.pallas_call(
        kernel,
        out_shape=jax.ShapeDtypeStruct((ROWS, D), bf),
        in_specs=[smem] * 2 + [hbm] * 4,
        out_specs=pl.BlockSpec(memory_space=pltpu.VMEM),
        scratch_shapes=[
            pltpu.VMEM((ROWS, D), bf),
            pltpu.VMEM((D, 4 * D), bf),
            pltpu.VMEM((D, D), bf),
            pltpu.VMEM((2, HIST, D), bf),
            [pltpu.VMEM((4, 2, R, 2 * HD), bf)] * NQ,
            pltpu.VMEM((4, NQ, 2, 2, R, HD), bf),
            [pltpu.VMEM((4, 2, 2, w, HD), bf) for w in WIDE],
            [pltpu.VMEM((2, 2, 16, w, HD), bf) for w in WIDE],
            pltpu.VMEM((ROWS, 4 * D), bf),
            pltpu.VMEM((8, ROWS, HD), bf),
            pltpu.VMEM((8, ROWS, HD), jnp.float32),
            pltpu.VMEM((8, ROWS, HD), bf),
            pltpu.VMEM((8, ROWS, HD), bf),
            pltpu.VMEM((ROWS, D), jnp.float32),
            dma((4,)),
            dma((4,)),
            dma,
            dma((NQ,)),
            dma,
            dma((NQ,)),
            dma,
            dma((NS,)),
            dma,
            dma((NS,)),
            dma,
            dma,
            dma,
            dma,
            pltpu.SemaphoreType.REGULAR,
        ],
        compiler_params=pltpu.CompilerParams(
            collective_id=0, has_side_effects=True, vmem_limit_bytes=60 * 2**20
        ),
    )(
        user_slot, hist_len,
        cand_x.reshape(ROWS, D), f1_weight, out_weight, kv_cache.reshape(HIST, 2 * D),
    )
    count = cand_count[lax.axis_index("group")]
    ids = lax.axis_index("pos") * ROWS + jnp.arange(ROWS, dtype=jnp.int32)
    return jnp.where((ids < count)[None, :, None], out.reshape(1, ROWS, D), jnp.bfloat16(0))


def solution(mesh):
    placed = (P("group", "pos", None), P(), P(), P("group", "pos", None), P(), P(), P())
    return jax.shard_map(
        body, mesh=mesh, in_specs=placed, out_specs=P("group", "pos", None), check_vma=False
    )
```

```python
import math

import jax
import jax.numpy as jnp
from jax import lax
from jax.experimental import pallas as pl
from jax.experimental.pallas import tpu as pltpu
from jax.sharding import PartitionSpec as P

MESH = pl.DeviceIdType.MESH
HEADS = 8
HD = 128
D = 1024
ROWS = 512
HIST = 128
NQ = 4
R = HIST // NQ
SPANS = ((0, 1), (1, 2), (2, 4))
NS = len(SPANS)
LAST = NS - 1
WIDE = [(b - a) * R for a, b in SPANS]
COLS = 256
SPREAD = (10, 2, 8, 6, 14, 9, 11, 5, 7, 13, 15, 1, 3, 4, 12, 0)


def silu(v):
    h = 0.5 * v
    return h + h * jnp.tanh(h)


def wait_bytes(ref, sem):
    pltpu.make_async_copy(ref, ref, sem).wait()


def kernel(
    slot_ref, len_ref, count_ref, x_hbm, f1_hbm, ow_hbm, kv_hbm, out_ref,
    xv, f1v, owv, kvin, st1, st2, sel, kvbuf, projv, qbuf, acc, asend, abuf, selfv,
    load_sem, f1_sem, s1s, s1r, s2s, s2r, s3s, s3r, xs, xr, qs, qr, os, orr,
    in_plane,
):
    y = lax.axis_index("group")
    pos = lax.axis_index("pos")
    c = lax.rem(pos, 2)
    z = lax.rem(pos // 2, 4)
    x = pos // 8
    chip = x * 4 + z

    def at(xx, zz, cc):
        return (xx * 4 + zz) * 2 + cc

    def head_at(xx, zz):
        a = lax.rem(xx + 4 - zz, 4)
        return (lax.rem(a, 2) * 2 + lax.rem(xx, 2)) * 2 + a // 2

    mine = head_at(x, z)
    offsets = [
        (1 + 2 * c, 1 + 2 * c), (1 + 2 * c, 3 - 2 * c), (2 - 2 * c, 2 * c),
        (1, 0), (3, 0), (0, 1), (0, 3), (0, 0),
    ]

    kv_loads = [
        pltpu.make_async_copy(kv_hbm.at[:, pl.ds(i * D, D)], kvin.at[i], load_sem.at[i]) for i in range(2)
    ]
    for cp in kv_loads:
        cp.start()
    x_load = pltpu.make_async_copy(x_hbm, xv, load_sem.at[2])
    x_load.start()
    f1_loads = {}
    for i in (2, 3, 1, 0):
        cols = pl.ds(i * D, D)
        f1_loads[i] = pltpu.make_async_copy(f1_hbm.at[:, cols], f1v.at[:, cols], f1_sem.at[i])
        f1_loads[i].start()
    ow_load = pltpu.make_async_copy(ow_hbm, owv, load_sem.at[3])
    ow_load.start()

    barrier = pltpu.get_barrier_semaphore()

    def greet(sem, g, p):
        pl.semaphore_signal(sem, inc=1, device_id=(g, p), device_id_type=MESH)

    def greet_x(sem):
        for d in range(1, 4):
            greet(sem, y, at(lax.rem(x + d, 4), z, c))

    def greet_y(sem):
        for d in range(1, 4):
            greet(sem, lax.rem(y + d, 4), pos)

    greet_y(barrier)
    greet_x(barrier)
    for d in range(1, 4):
        greet(barrier, y, at(x, lax.rem(z + d, 4), c))
    greet(barrier, y, at(x, z, 1 - c))
    def project(i):
        f1_loads[i].wait()

        def tile(n, carry):
            cols = pl.ds(pl.multiple_of(i * D + n * COLS, COLS), COLS)
            v = jnp.dot(xv[...], f1v[:, cols], preferred_element_type=jnp.float32)
            projv[:, cols] = silu(v).astype(jnp.bfloat16)
            return carry

        lax.fori_loop(0, D // COLS, tile, 0)

    x_load.wait()
    project(2)
    pl.semaphore_wait(barrier, 10)

    for cp in kv_loads:
        cp.wait()

    def pair_cols(yy):
        return pl.ds(pl.multiple_of(yy * 256, 256), 256)

    for q in range(NQ):
        rows = pl.ds(q * R, R)
        for d in (2, 1, 3):
            yy = lax.rem(y + d, 4)
            pltpu.make_async_remote_copy(
                src_ref=kvin.at[:, rows, pair_cols(yy)],
                dst_ref=st1[q].at[y],
                send_sem=s1s,
                recv_sem=s1r.at[q],
                device_id=(yy, pos),
                device_id_type=MESH,
            ).start()
        st1[q][y] = kvin[:, rows, pair_cols(y)]

    greet_x(in_plane)
    project(3)
    pl.semaphore_wait(in_plane, 3)


    def head_cols(base, head):
        return pl.ds(pl.multiple_of(base * D + head * HD, HD), HD)

    for k in range(7):
        xx, zz = lax.rem(x + offsets[k][0], 4), lax.rem(z + offsets[k][1], 4)
        pltpu.make_async_remote_copy(
            src_ref=projv.at[:, head_cols(2, head_at(xx, zz))],
            dst_ref=qbuf.at[k],
            send_sem=qs,
            recv_sem=qr,
            device_id=(y, at(xx, zz, c)),
            device_id_type=MESH,
        ).start()
    qbuf[7] = projv[:, head_cols(2, mine)]

    def stage2(q):
        wait_bytes(st1[q].at[pl.ds(0, 3)], s1r.at[q])
        g = [i for i in range(NS) if SPANS[i][0] <= q < SPANS[i][1]][0]
        rows = pl.ds((q - SPANS[g][0]) * R, R)
        for r in range(4):
            s = slot_ref[r]
            live = (pos * HIST < len_ref[r]).astype(jnp.bfloat16)
            both = st1[q][s]
            for j in range(2):
                st2[r, q, j, 0] = both[0, :, j * HD : (j + 1) * HD]
                st2[r, q, j, 1] = both[1, :, j * HD : (j + 1) * HD] * live
        for d in (2, 1, 3):
            r = lax.rem(y + d, 4)
            pltpu.make_async_remote_copy(
                src_ref=st2.at[r, q],
                dst_ref=sel[g].at[y, :, :, rows, :],
                send_sem=s2s,
                recv_sem=s2r.at[q],
                device_id=(r, pos),
                device_id_type=MESH,
            ).start()
        sel[g][y, :, :, rows, :] = st2[y, q]

    def stage3(g):
        for q in range(*SPANS[g]):
            wait_bytes(st2.at[pl.ds(0, 3), q], s2r.at[q])
        for d in SPREAD:
            xx, zz = lax.rem(x + d // 4, 4), lax.rem(z + d % 4, 4)
            h = head_at(xx, zz)
            src = sel[g].at[h // 2, lax.rem(h, 2)]
            dst = kvbuf[g].at[:, c, chip]
            if d == 0:
                pltpu.make_async_copy(src, dst, s3r.at[g]).start()
            else:
                pltpu.make_async_remote_copy(
                    src_ref=src,
                    dst_ref=dst,
                    send_sem=s3s,
                    recv_sem=s3r.at[g],
                    device_id=(y, at(xx, zz, c)),
                    device_id_type=MESH,
                ).start()

    def share(g):
        wait_bytes(kvbuf[g].at[:, c], s3r.at[g])
        pltpu.make_async_remote_copy(
            src_ref=kvbuf[g].at[:, c],
            dst_ref=kvbuf[g].at[:, c],
            send_sem=xs,
            recv_sem=xr.at[g],
            device_id=(y, at(x, z, 1 - c)),
            device_id_type=MESH,
        ).start()

    denom = (len_ref[y] + 1).astype(jnp.float32)
    scale = 1.0 / math.sqrt(HD)

    def own_term():
        def tile(n, carry):
            rows = pl.ds(pl.multiple_of(n * 128, 128), 128)
            for h in range(HEADS):
                lo = h * HD
                qh = projv[rows, 2 * D + lo : 2 * D + lo + HD].astype(jnp.float32)
                kh = projv[rows, 3 * D + lo : 3 * D + lo + HD].astype(jnp.float32)
                vh = projv[rows, D + lo : D + lo + HD].astype(jnp.float32)
                score = jnp.sum(qh * kh, axis=-1, keepdims=True) * scale
                weight = (silu(score) / denom).astype(jnp.bfloat16).astype(jnp.float32)
                selfv[rows, lo : lo + HD] = weight * vh
            return carry

        lax.fori_loop(0, ROWS // 128, tile, 0)

    stage2(0)
    stage2(1)
    project(1)
    stage3(0)
    stage2(2)
    project(0)
    stage3(1)
    stage2(3)
    own_term()
    stage3(2)

    def attend(g, half, qv):
        k = kvbuf[g][0, half].reshape(16 * WIDE[g], HD)
        v = kvbuf[g][1, half].reshape(16 * WIDE[g], HD)
        s = lax.dot_general(qv, k, (((1,), (1,)), ((), ())), preferred_element_type=jnp.float32)
        w = silu(s * scale).astype(jnp.bfloat16)
        return jnp.dot(w, v, preferred_element_type=jnp.float32)

    def attend_all(g, half, first):
        count = 8 if WIDE[g] == R else 4

        def block(b, carry):
            part = pl.ds(b * count, count)
            o = attend(g, half, qbuf[part].reshape(count * ROWS, HD)).reshape(count, ROWS, HD)
            if first:
                acc[part] = o
            else:
                acc[part] += o
            return carry

        lax.fori_loop(0, 8 // count, block, 0)

    for g in range(LAST):
        share(g)
        if g == 0:
            wait_bytes(qbuf.at[pl.ds(0, 7)], qr)
        attend_all(g, c, g == 0)
        wait_bytes(kvbuf[g].at[:, 1 - c], xr.at[g])
        attend_all(g, 1 - c, False)

    share(LAST)
    wait_bytes(kvbuf[LAST].at[:, 1 - c], xr.at[LAST])
    steps_x = sum(v * 4**i for i, v in enumerate((1, 1, 2, 1, 3, 0, 0, 0)))
    steps_x = steps_x + c * (sum(v * 4**i for i, v in enumerate((3, 3, 0, 1, 3, 0, 0, 0))) - steps_x)
    steps_z = sum(v * 4**i for i, v in enumerate((1, 3, 0, 0, 0, 1, 3, 0)))
    steps_z = steps_z + c * (sum(v * 4**i for i, v in enumerate((3, 1, 2, 0, 0, 1, 3, 0))) - steps_z)

    def last(k, place):
        qv = qbuf[k]
        o = (acc[k] + attend(LAST, 0, qv) + attend(LAST, 1, qv)) / denom
        asend[k] = o.astype(jnp.bfloat16)
        xx = lax.rem(x + 4 - lax.rem(steps_x // place, 4), 4)
        zz = lax.rem(z + 4 - lax.rem(steps_z // place, 4), 4)

        @pl.when(k < 7)
        def _():
            pltpu.make_async_remote_copy(
                src_ref=asend.at[k],
                dst_ref=abuf.at[mine],
                send_sem=os,
                recv_sem=orr,
                device_id=(y, at(xx, zz, c)),
                device_id_type=MESH,
            ).start()

        return place * 4

    lax.fori_loop(0, 8, last, 1)
    abuf[mine] = asend[7]

    ow_load.wait()
    wait_bytes(abuf.at[pl.ds(0, 7)], orr)
    count = count_ref[y]

    def finish(n, carry):
        rows = pl.ds(pl.multiple_of(n * 128, 128), 128)
        attn = jnp.concatenate([abuf[h, rows, :] for h in range(HEADS)], axis=-1).astype(jnp.float32)
        attn = attn + selfv[rows, :]
        mean = jnp.mean(attn, axis=-1, keepdims=True)
        centered = attn - mean
        var = jnp.mean(centered * centered, axis=-1, keepdims=True)
        normed = centered * lax.rsqrt(var + 1e-05)
        mixed = (normed * projv[rows, 0:D].astype(jnp.float32)).astype(jnp.bfloat16)
        result = xv[rows, :].astype(jnp.float32) + jnp.dot(mixed, owv[...], preferred_element_type=jnp.float32)
        ids = pos * ROWS + n * 128 + lax.broadcasted_iota(jnp.int32, (128, 1), 0)
        out_ref[rows, :] = jnp.where(ids < count, result, 0.0).astype(jnp.bfloat16)
        return carry

    lax.fori_loop(0, ROWS // 128, finish, 0)

    for q in range(NQ):
        wait_bytes(st1[q].at[pl.ds(0, 3)], s1s)
    wait_bytes(qbuf.at[pl.ds(0, 7)], qs)

    wait_bytes(st2.at[pl.ds(0, 3)], s2s)
    for g in range(NS):
        wait_bytes(kvbuf[g].at[:, 0, pl.ds(0, 15)], s3s)
        wait_bytes(kvbuf[g].at[:, 0], xs)
    wait_bytes(abuf.at[pl.ds(0, 7)], os)


def body(cand_x, f1_weight, out_weight, kv_cache, user_slot, hist_len, cand_count):
    bf = jnp.bfloat16
    smem = pl.BlockSpec(memory_space=pltpu.SMEM)
    hbm = pl.BlockSpec(memory_space=pl.ANY)
    dma = pltpu.SemaphoreType.DMA
    out = pl.pallas_call(
        kernel,
        out_shape=jax.ShapeDtypeStruct((ROWS, D), bf),
        in_specs=[smem] * 3 + [hbm] * 4,
        out_specs=pl.BlockSpec(memory_space=pltpu.VMEM),
        scratch_shapes=[
            pltpu.VMEM((ROWS, D), bf),
            pltpu.VMEM((D, 4 * D), bf),
            pltpu.VMEM((D, D), bf),
            pltpu.VMEM((2, HIST, D), bf),
            [pltpu.VMEM((4, 2, R, 2 * HD), bf)] * NQ,
            pltpu.VMEM((4, NQ, 2, 2, R, HD), bf),
            [pltpu.VMEM((4, 2, 2, w, HD), bf) for w in WIDE],
            [pltpu.VMEM((2, 2, 16, w, HD), bf) for w in WIDE],
            pltpu.VMEM((ROWS, 4 * D), bf),
            pltpu.VMEM((8, ROWS, HD), bf),
            pltpu.VMEM((8, ROWS, HD), jnp.float32),
            pltpu.VMEM((8, ROWS, HD), bf),
            pltpu.VMEM((8, ROWS, HD), bf),
            pltpu.VMEM((ROWS, D), jnp.float32),
            dma((4,)),
            dma((4,)),
            dma,
            dma((NQ,)),
            dma,
            dma((NQ,)),
            dma,
            dma((NS,)),
            dma,
            dma((NS,)),
            dma,
            dma,
            dma,
            dma,
            pltpu.SemaphoreType.REGULAR,
        ],
        compiler_params=pltpu.CompilerParams(
            collective_id=0, has_side_effects=True, vmem_limit_bytes=60 * 2**20
        ),
    )(
        user_slot, hist_len, cand_count,
        cand_x.reshape(ROWS, D), f1_weight, out_weight, kv_cache.reshape(HIST, 2 * D),
    )
    return out.reshape(1, ROWS, D)


def solution(mesh):
    placed = (P("group", "pos", None), P(), P(), P("group", "pos", None), P(), P(), P())
    return jax.shard_map(
        body, mesh=mesh, in_specs=placed, out_specs=P("group", "pos", None), check_vma=False
    )
```

```python
import math

import jax
import jax.numpy as jnp
from jax import lax
from jax.experimental import pallas as pl
from jax.experimental.pallas import tpu as pltpu
from jax.sharding import PartitionSpec as P

MESH = pl.DeviceIdType.MESH
HEADS = 8
HD = 128
D = 1024
ROWS = 512
HIST = 128
NQ = 4
R = HIST // NQ
SPANS = ((0, 1), (1, 2), (2, 4))
NS = len(SPANS)
LAST = NS - 1
WIDE = [(b - a) * R for a, b in SPANS]
COLS = 256
SPREAD = (10, 2, 8, 6, 14, 9, 11, 5, 7, 13, 15, 1, 3, 4, 12, 0)


def silu(v):
    h = 0.5 * v
    return h + h * jnp.tanh(h)


def wait_bytes(ref, sem):
    pltpu.make_async_copy(ref, ref, sem).wait()


def kernel(
    slot_ref, len_ref, count_ref, x_hbm, f1_hbm, ow_hbm, kv_hbm, out_ref,
    xv, f1v, owv, kvin, st1, st2, sel, kvbuf, projv, qbuf, acc, asend, abuf, selfv,
    load_sem, f1_sem, s1s, s1r, s2s, s2r, s3s, s3r, xs, xr, qs, qr, os, orr,
    in_plane,
):
    y = lax.axis_index("group")
    pos = lax.axis_index("pos")
    c = lax.rem(pos, 2)
    z = lax.rem(pos // 2, 4)
    x = pos // 8
    chip = x * 4 + z

    def at(xx, zz, cc):
        return (xx * 4 + zz) * 2 + cc

    def head_at(xx, zz):
        a = lax.rem(xx + 4 - zz, 4)
        return (lax.rem(a, 2) * 2 + lax.rem(xx, 2)) * 2 + a // 2

    mine = head_at(x, z)
    offsets = [
        (1 + 2 * c, 1 + 2 * c), (1 + 2 * c, 3 - 2 * c), (2 - 2 * c, 2 * c),
        (1, 0), (3, 0), (0, 1), (0, 3), (0, 0),
    ]

    kv_loads = [
        pltpu.make_async_copy(kv_hbm.at[:, pl.ds(i * D, D)], kvin.at[i], load_sem.at[i]) for i in range(2)
    ]
    for cp in kv_loads:
        cp.start()
    x_load = pltpu.make_async_copy(x_hbm, xv, load_sem.at[2])
    x_load.start()
    f1_loads = {}
    for i in (2, 3, 1, 0):
        cols = pl.ds(i * D, D)
        f1_loads[i] = pltpu.make_async_copy(f1_hbm.at[:, cols], f1v.at[:, cols], f1_sem.at[i])
        f1_loads[i].start()
    ow_load = pltpu.make_async_copy(ow_hbm, owv, load_sem.at[3])
    ow_load.start()

    barrier = pltpu.get_barrier_semaphore()

    def greet(sem, g, p):
        pl.semaphore_signal(sem, inc=1, device_id=(g, p), device_id_type=MESH)

    def greet_x(sem):
        for d in range(1, 4):
            greet(sem, y, at(lax.rem(x + d, 4), z, c))

    def greet_y(sem):
        for d in range(1, 4):
            greet(sem, lax.rem(y + d, 4), pos)

    greet_y(barrier)
    greet_x(barrier)
    for d in range(1, 4):
        greet(barrier, y, at(x, lax.rem(z + d, 4), c))
    greet(barrier, y, at(x, z, 1 - c))
    pl.semaphore_wait(barrier, 10)

    for cp in kv_loads:
        cp.wait()

    def pair_cols(yy):
        return pl.ds(pl.multiple_of(yy * 256, 256), 256)

    for q in range(NQ):
        rows = pl.ds(q * R, R)
        for d in (2, 1, 3):
            yy = lax.rem(y + d, 4)
            pltpu.make_async_remote_copy(
                src_ref=kvin.at[:, rows, pair_cols(yy)],
                dst_ref=st1[q].at[y],
                send_sem=s1s,
                recv_sem=s1r.at[q],
                device_id=(yy, pos),
                device_id_type=MESH,
            ).start()
        st1[q][y] = kvin[:, rows, pair_cols(y)]

    greet_x(in_plane)

    def project(i):
        f1_loads[i].wait()

        def tile(n, carry):
            cols = pl.ds(pl.multiple_of(i * D + n * COLS, COLS), COLS)
            v = jnp.dot(xv[...], f1v[:, cols], preferred_element_type=jnp.float32)
            projv[:, cols] = silu(v).astype(jnp.bfloat16)
            return carry

        lax.fori_loop(0, D // COLS, tile, 0)

    x_load.wait()
    project(2)
    pl.semaphore_wait(in_plane, 3)

    def head_cols(base, head):
        return pl.ds(pl.multiple_of(base * D + head * HD, HD), HD)

    for k in range(7):
        xx, zz = lax.rem(x + offsets[k][0], 4), lax.rem(z + offsets[k][1], 4)
        pltpu.make_async_remote_copy(
            src_ref=projv.at[:, head_cols(2, head_at(xx, zz))],
            dst_ref=qbuf.at[k],
            send_sem=qs,
            recv_sem=qr,
            device_id=(y, at(xx, zz, c)),
            device_id_type=MESH,
        ).start()
    qbuf[7] = projv[:, head_cols(2, mine)]

    def stage2(q):
        wait_bytes(st1[q].at[pl.ds(0, 3)], s1r.at[q])
        g = [i for i in range(NS) if SPANS[i][0] <= q < SPANS[i][1]][0]
        rows = pl.ds((q - SPANS[g][0]) * R, R)
        for d in (2, 1, 3, 0):
            r = lax.rem(y + d, 4)
            s = slot_ref[r]
            live = (pos * HIST < len_ref[r]).astype(jnp.bfloat16)
            both = st1[q][s]
            for j in range(2):
                st2[r, q, j, 0] = both[0, :, j * HD : (j + 1) * HD]
                st2[r, q, j, 1] = both[1, :, j * HD : (j + 1) * HD] * live
            if d:
                pltpu.make_async_remote_copy(
                    src_ref=st2.at[r, q],
                    dst_ref=sel[g].at[y, :, :, rows, :],
                    send_sem=s2s,
                    recv_sem=s2r.at[q],
                    device_id=(r, pos),
                    device_id_type=MESH,
                ).start()
        sel[g][y, :, :, rows, :] = st2[y, q]

    def stage3(g):
        for q in range(*SPANS[g]):
            wait_bytes(st2.at[pl.ds(0, 3), q], s2r.at[q])
        for d in SPREAD:
            xx, zz = lax.rem(x + d // 4, 4), lax.rem(z + d % 4, 4)
            h = head_at(xx, zz)
            src = sel[g].at[h // 2, lax.rem(h, 2)]
            dst = kvbuf[g].at[:, c, chip]
            if d == 0:
                pltpu.make_async_copy(src, dst, s3r.at[g]).start()
            else:
                pltpu.make_async_remote_copy(
                    src_ref=src,
                    dst_ref=dst,
                    send_sem=s3s,
                    recv_sem=s3r.at[g],
                    device_id=(y, at(xx, zz, c)),
                    device_id_type=MESH,
                ).start()

    def share(g):
        wait_bytes(kvbuf[g].at[:, c], s3r.at[g])
        pltpu.make_async_remote_copy(
            src_ref=kvbuf[g].at[:, c],
            dst_ref=kvbuf[g].at[:, c],
            send_sem=xs,
            recv_sem=xr.at[g],
            device_id=(y, at(x, z, 1 - c)),
            device_id_type=MESH,
        ).start()

    denom = (len_ref[y] + 1).astype(jnp.float32)
    scale = 1.0 / math.sqrt(HD)

    def own_term():
        def tile(n, carry):
            rows = pl.ds(pl.multiple_of(n * 128, 128), 128)
            for h in range(HEADS):
                lo = h * HD
                qh = projv[rows, 2 * D + lo : 2 * D + lo + HD].astype(jnp.float32)
                kh = projv[rows, 3 * D + lo : 3 * D + lo + HD].astype(jnp.float32)
                vh = projv[rows, D + lo : D + lo + HD].astype(jnp.float32)
                score = jnp.sum(qh * kh, axis=-1, keepdims=True) * scale
                weight = (silu(score) / denom).astype(jnp.bfloat16).astype(jnp.float32)
                selfv[rows, lo : lo + HD] = weight * vh
            return carry

        lax.fori_loop(0, ROWS // 128, tile, 0)

    pieces = [lambda: project(3), lambda: project(1), lambda: project(0), own_term]
    ready = [b for a, b in SPANS]
    stage2(0)
    done = 0
    for q in range(1, NQ):
        stage2(q)
        for piece in pieces[(q - 1) * 4 // (NQ - 1) : q * 4 // (NQ - 1)]:
            piece()
        if ready[done] <= q:
            stage3(done)
            done += 1
    while done < NS:
        stage3(done)
        done += 1

    def attend(g, half, qv):
        k = kvbuf[g][0, half].reshape(16 * WIDE[g], HD)
        v = kvbuf[g][1, half].reshape(16 * WIDE[g], HD)
        s = lax.dot_general(qv, k, (((1,), (1,)), ((), ())), preferred_element_type=jnp.float32)
        w = silu(s * scale).astype(jnp.bfloat16)
        return jnp.dot(w, v, preferred_element_type=jnp.float32)

    def attend_all(g, half, first):
        count = 8 if WIDE[g] == R else 4

        def block(b, carry):
            part = pl.ds(b * count, count)
            o = attend(g, half, qbuf[part].reshape(count * ROWS, HD)).reshape(count, ROWS, HD)
            if first:
                acc[part] = o
            else:
                acc[part] += o
            return carry

        lax.fori_loop(0, 8 // count, block, 0)

    for g in range(LAST):
        share(g)
        if g == 0:
            wait_bytes(qbuf.at[pl.ds(0, 7)], qr)
        attend_all(g, c, g == 0)
        wait_bytes(kvbuf[g].at[:, 1 - c], xr.at[g])
        attend_all(g, 1 - c, False)

    share(LAST)
    wait_bytes(kvbuf[LAST].at[:, 1 - c], xr.at[LAST])
    steps_x = sum(v * 4**i for i, v in enumerate((1, 1, 2, 1, 3, 0, 0, 0)))
    steps_x = steps_x + c * (sum(v * 4**i for i, v in enumerate((3, 3, 0, 1, 3, 0, 0, 0))) - steps_x)
    steps_z = sum(v * 4**i for i, v in enumerate((1, 3, 0, 0, 0, 1, 3, 0)))
    steps_z = steps_z + c * (sum(v * 4**i for i, v in enumerate((3, 1, 2, 0, 0, 1, 3, 0))) - steps_z)

    def last(k, place):
        qv = qbuf[k]
        o = (acc[k] + attend(LAST, 0, qv) + attend(LAST, 1, qv)) / denom
        asend[k] = o.astype(jnp.bfloat16)
        xx = lax.rem(x + 4 - lax.rem(steps_x // place, 4), 4)
        zz = lax.rem(z + 4 - lax.rem(steps_z // place, 4), 4)

        @pl.when(k < 7)
        def _():
            pltpu.make_async_remote_copy(
                src_ref=asend.at[k],
                dst_ref=abuf.at[mine],
                send_sem=os,
                recv_sem=orr,
                device_id=(y, at(xx, zz, c)),
                device_id_type=MESH,
            ).start()

        return place * 4

    lax.fori_loop(0, 8, last, 1)
    abuf[mine] = asend[7]

    ow_load.wait()
    wait_bytes(abuf.at[pl.ds(0, 7)], orr)
    count = count_ref[y]

    def finish(n, carry):
        rows = pl.ds(pl.multiple_of(n * 128, 128), 128)
        attn = jnp.concatenate([abuf[h, rows, :] for h in range(HEADS)], axis=-1).astype(jnp.float32)
        attn = attn + selfv[rows, :]
        mean = jnp.mean(attn, axis=-1, keepdims=True)
        centered = attn - mean
        var = jnp.mean(centered * centered, axis=-1, keepdims=True)
        normed = centered * lax.rsqrt(var + 1e-05)
        mixed = (normed * projv[rows, 0:D].astype(jnp.float32)).astype(jnp.bfloat16)
        result = xv[rows, :].astype(jnp.float32) + jnp.dot(mixed, owv[...], preferred_element_type=jnp.float32)
        ids = pos * ROWS + n * 128 + lax.broadcasted_iota(jnp.int32, (128, 1), 0)
        out_ref[rows, :] = jnp.where(ids < count, result, 0.0).astype(jnp.bfloat16)
        return carry

    lax.fori_loop(0, ROWS // 128, finish, 0)

    for q in range(NQ):
        wait_bytes(st1[q].at[pl.ds(0, 3)], s1s)
    wait_bytes(qbuf.at[pl.ds(0, 7)], qs)

    wait_bytes(st2.at[pl.ds(0, 3)], s2s)
    for g in range(NS):
        wait_bytes(kvbuf[g].at[:, 0, pl.ds(0, 15)], s3s)
        wait_bytes(kvbuf[g].at[:, 0], xs)
    wait_bytes(abuf.at[pl.ds(0, 7)], os)


def body(cand_x, f1_weight, out_weight, kv_cache, user_slot, hist_len, cand_count):
    bf = jnp.bfloat16
    smem = pl.BlockSpec(memory_space=pltpu.SMEM)
    hbm = pl.BlockSpec(memory_space=pl.ANY)
    dma = pltpu.SemaphoreType.DMA
    out = pl.pallas_call(
        kernel,
        out_shape=jax.ShapeDtypeStruct((ROWS, D), bf),
        in_specs=[smem] * 3 + [hbm] * 4,
        out_specs=pl.BlockSpec(memory_space=pltpu.VMEM),
        scratch_shapes=[
            pltpu.VMEM((ROWS, D), bf),
            pltpu.VMEM((D, 4 * D), bf),
            pltpu.VMEM((D, D), bf),
            pltpu.VMEM((2, HIST, D), bf),
            [pltpu.VMEM((4, 2, R, 2 * HD), bf)] * NQ,
            pltpu.VMEM((4, NQ, 2, 2, R, HD), bf),
            [pltpu.VMEM((4, 2, 2, w, HD), bf) for w in WIDE],
            [pltpu.VMEM((2, 2, 16, w, HD), bf) for w in WIDE],
            pltpu.VMEM((ROWS, 4 * D), bf),
            pltpu.VMEM((8, ROWS, HD), bf),
            pltpu.VMEM((8, ROWS, HD), jnp.float32),
            pltpu.VMEM((8, ROWS, HD), bf),
            pltpu.VMEM((8, ROWS, HD), bf),
            pltpu.VMEM((ROWS, D), jnp.float32),
            dma((4,)),
            dma((4,)),
            dma,
            dma((NQ,)),
            dma,
            dma((NQ,)),
            dma,
            dma((NS,)),
            dma,
            dma((NS,)),
            dma,
            dma,
            dma,
            dma,
            pltpu.SemaphoreType.REGULAR,
        ],
        compiler_params=pltpu.CompilerParams(
            collective_id=0, has_side_effects=True, vmem_limit_bytes=60 * 2**20
        ),
    )(
        user_slot, hist_len, cand_count,
        cand_x.reshape(ROWS, D), f1_weight, out_weight, kv_cache.reshape(HIST, 2 * D),
    )
    return out.reshape(1, ROWS, D)


def solution(mesh):
    placed = (P("group", "pos", None), P(), P(), P("group", "pos", None), P(), P(), P())
    return jax.shard_map(
        body, mesh=mesh, in_specs=placed, out_specs=P("group", "pos", None), check_vma=False
    )
```

```python
import math

import jax
import jax.numpy as jnp
from jax import lax
from jax.experimental import pallas as pl
from jax.experimental.pallas import tpu as pltpu
from jax.sharding import PartitionSpec as P

MESH = pl.DeviceIdType.MESH
HEADS = 8
HD = 128
D = 1024
ROWS = 512
HIST = 128
NQ = 4
R = HIST // NQ
SPANS = ((0, 1), (1, 2), (2, 4))
NS = len(SPANS)
LAST = NS - 1
WIDE = [(b - a) * R for a, b in SPANS]
COLS = 256
SPREAD = (10, 2, 8, 6, 14, 9, 11, 5, 7, 13, 15, 1, 3, 4, 12, 0)


def silu(v):
    h = 0.5 * v
    return h + h * jnp.tanh(h)


def wait_bytes(ref, sem):
    pltpu.make_async_copy(ref, ref, sem).wait()


def kernel(
    slot_ref, len_ref, count_ref, x_hbm, f1_hbm, ow_hbm, kv_hbm, out_ref,
    xv, f1v, owv, kvin, st1, st2, sel, kvbuf, projv, qbuf, acc, asend, abuf, selfv,
    load_sem, f1_sem, s1s, s1r, s2s, s2r, s3s, s3r, xs, xr, qs, qr, os, orr,
    in_plane,
):
    y = lax.axis_index("group")
    pos = lax.axis_index("pos")
    c = lax.rem(pos, 2)
    z = lax.rem(pos // 2, 4)
    x = pos // 8
    chip = x * 4 + z

    def at(xx, zz, cc):
        return (xx * 4 + zz) * 2 + cc

    def head_at(xx, zz):
        a = lax.rem(xx + 4 - zz, 4)
        return (lax.rem(a, 2) * 2 + lax.rem(xx, 2)) * 2 + a // 2

    mine = head_at(x, z)
    offsets = [
        (1 + 2 * c, 1 + 2 * c), (1 + 2 * c, 3 - 2 * c), (2 - 2 * c, 2 * c),
        (1, 0), (3, 0), (0, 1), (0, 3), (0, 0),
    ]

    kv_loads = [
        pltpu.make_async_copy(kv_hbm.at[:, pl.ds(i * D, D)], kvin.at[i], load_sem.at[i]) for i in range(2)
    ]
    for cp in kv_loads:
        cp.start()
    x_load = pltpu.make_async_copy(x_hbm, xv, load_sem.at[2])
    x_load.start()
    f1_loads = {}
    for i in (2, 3, 1, 0):
        cols = pl.ds(i * D, D)
        f1_loads[i] = pltpu.make_async_copy(f1_hbm.at[:, cols], f1v.at[:, cols], f1_sem.at[i])
        f1_loads[i].start()
    ow_load = pltpu.make_async_copy(ow_hbm, owv, load_sem.at[3])
    ow_load.start()

    barrier = pltpu.get_barrier_semaphore()

    def greet(sem, g, p):
        pl.semaphore_signal(sem, inc=1, device_id=(g, p), device_id_type=MESH)

    def greet_x(sem):
        for d in range(1, 4):
            greet(sem, y, at(lax.rem(x + d, 4), z, c))

    def greet_y(sem):
        for d in range(1, 4):
            greet(sem, lax.rem(y + d, 4), pos)

    greet_y(barrier)
    greet_x(barrier)
    for d in range(1, 4):
        greet(barrier, y, at(x, lax.rem(z + d, 4), c))
    greet(barrier, y, at(x, z, 1 - c))
    pl.semaphore_wait(barrier, 10)

    for cp in kv_loads:
        cp.wait()

    def pair_cols(yy):
        return pl.ds(pl.multiple_of(yy * 256, 256), 256)

    for q in range(NQ):
        rows = pl.ds(q * R, R)
        for d in (2, 1, 3):
            yy = lax.rem(y + d, 4)
            pltpu.make_async_remote_copy(
                src_ref=kvin.at[:, rows, pair_cols(yy)],
                dst_ref=st1[q].at[y],
                send_sem=s1s,
                recv_sem=s1r.at[q],
                device_id=(yy, pos),
                device_id_type=MESH,
            ).start()
        st1[q][y] = kvin[:, rows, pair_cols(y)]

    greet_x(in_plane)

    def project(i):
        f1_loads[i].wait()

        def tile(n, carry):
            cols = pl.ds(pl.multiple_of(i * D + n * COLS, COLS), COLS)
            v = jnp.dot(xv[...], f1v[:, cols], preferred_element_type=jnp.float32)
            projv[:, cols] = silu(v).astype(jnp.bfloat16)
            return carry

        lax.fori_loop(0, D // COLS, tile, 0)

    x_load.wait()
    project(2)
    pl.semaphore_wait(in_plane, 3)

    def head_cols(base, head):
        return pl.ds(pl.multiple_of(base * D + head * HD, HD), HD)

    for k in range(7):
        xx, zz = lax.rem(x + offsets[k][0], 4), lax.rem(z + offsets[k][1], 4)
        pltpu.make_async_remote_copy(
            src_ref=projv.at[:, head_cols(2, head_at(xx, zz))],
            dst_ref=qbuf.at[k],
            send_sem=qs,
            recv_sem=qr,
            device_id=(y, at(xx, zz, c)),
            device_id_type=MESH,
        ).start()
    qbuf[7] = projv[:, head_cols(2, mine)]

    def stage2(q):
        wait_bytes(st1[q].at[pl.ds(0, 3)], s1r.at[q])
        g = [i for i in range(NS) if SPANS[i][0] <= q < SPANS[i][1]][0]
        rows = pl.ds((q - SPANS[g][0]) * R, R)
        for d in (2, 1, 3, 0):
            r = lax.rem(y + d, 4)
            s = slot_ref[r]
            live = (pos * HIST < len_ref[r]).astype(jnp.bfloat16)
            both = st1[q][s]
            for j in range(2):
                st2[r, q, j, 0] = both[0, :, j * HD : (j + 1) * HD]
                st2[r, q, j, 1] = both[1, :, j * HD : (j + 1) * HD] * live
            if d:
                pltpu.make_async_remote_copy(
                    src_ref=st2.at[r, q],
                    dst_ref=sel[g].at[y, :, :, rows, :],
                    send_sem=s2s,
                    recv_sem=s2r.at[q],
                    device_id=(r, pos),
                    device_id_type=MESH,
                ).start()
        sel[g][y, :, :, rows, :] = st2[y, q]

    def stage3(g):
        for q in range(*SPANS[g]):
            wait_bytes(st2.at[pl.ds(0, 3), q], s2r.at[q])
        for d in SPREAD:
            xx, zz = lax.rem(x + d // 4, 4), lax.rem(z + d % 4, 4)
            h = head_at(xx, zz)
            src = sel[g].at[h // 2, lax.rem(h, 2)]
            dst = kvbuf[g].at[:, c, chip]
            if d == 0:
                pltpu.make_async_copy(src, dst, s3r.at[g]).start()
            else:
                pltpu.make_async_remote_copy(
                    src_ref=src,
                    dst_ref=dst,
                    send_sem=s3s,
                    recv_sem=s3r.at[g],
                    device_id=(y, at(xx, zz, c)),
                    device_id_type=MESH,
                ).start()

    def share(g):
        wait_bytes(kvbuf[g].at[:, c], s3r.at[g])
        pltpu.make_async_remote_copy(
            src_ref=kvbuf[g].at[:, c],
            dst_ref=kvbuf[g].at[:, c],
            send_sem=xs,
            recv_sem=xr.at[g],
            device_id=(y, at(x, z, 1 - c)),
            device_id_type=MESH,
        ).start()

    denom = (len_ref[y] + 1).astype(jnp.float32)
    scale = 1.0 / math.sqrt(HD)

    def own_term():
        def tile(n, carry):
            rows = pl.ds(pl.multiple_of(n * 128, 128), 128)
            for h in range(HEADS):
                lo = h * HD
                qh = projv[rows, 2 * D + lo : 2 * D + lo + HD].astype(jnp.float32)
                kh = projv[rows, 3 * D + lo : 3 * D + lo + HD].astype(jnp.float32)
                vh = projv[rows, D + lo : D + lo + HD].astype(jnp.float32)
                score = jnp.sum(qh * kh, axis=-1, keepdims=True) * scale
                weight = (silu(score) / denom).astype(jnp.bfloat16).astype(jnp.float32)
                selfv[rows, lo : lo + HD] = weight * vh
            return carry

        lax.fori_loop(0, ROWS // 128, tile, 0)

    pieces = [lambda: project(3), lambda: project(1), lambda: project(0), own_term]
    ready = [b for a, b in SPANS]
    stage2(0)
    done = 0
    for q in range(1, NQ):
        stage2(q)
        for piece in pieces[(q - 1) * 4 // (NQ - 1) : q * 4 // (NQ - 1)]:
            piece()
        if ready[done] <= q:
            stage3(done)
            done += 1
    while done < NS:
        stage3(done)
        done += 1

    def attend(g, half, qv):
        k = kvbuf[g][0, half].reshape(16 * WIDE[g], HD)
        v = kvbuf[g][1, half].reshape(16 * WIDE[g], HD)
        s = lax.dot_general(qv, k, (((1,), (1,)), ((), ())), preferred_element_type=jnp.float32)
        w = silu(s * scale).astype(jnp.bfloat16)
        return jnp.dot(w, v, preferred_element_type=jnp.float32)

    def attend_all(g, half, first):
        count = 8 if WIDE[g] == R else 4

        def block(b, carry):
            part = pl.ds(b * count, count)
            o = attend(g, half, qbuf[part].reshape(count * ROWS, HD)).reshape(count, ROWS, HD)
            if first:
                acc[part] = o
            else:
                acc[part] += o
            return carry

        lax.fori_loop(0, 8 // count, block, 0)

    for g in range(LAST):
        share(g)
        if g == 0:
            wait_bytes(qbuf.at[pl.ds(0, 7)], qr)
        attend_all(g, c, g == 0)
        wait_bytes(kvbuf[g].at[:, 1 - c], xr.at[g])
        attend_all(g, 1 - c, False)

    share(LAST)
    acc[0:4] += attend(LAST, c, qbuf[0:4].reshape(4 * ROWS, HD)).reshape(4, ROWS, HD)
    wait_bytes(kvbuf[LAST].at[:, 1 - c], xr.at[LAST])
    steps_x = sum(v * 4**i for i, v in enumerate((1, 1, 2, 1, 3, 0, 0, 0)))
    steps_x = steps_x + c * (sum(v * 4**i for i, v in enumerate((3, 3, 0, 1, 3, 0, 0, 0))) - steps_x)
    steps_z = sum(v * 4**i for i, v in enumerate((1, 3, 0, 0, 0, 1, 3, 0)))
    steps_z = steps_z + c * (sum(v * 4**i for i, v in enumerate((3, 1, 2, 0, 0, 1, 3, 0))) - steps_z)

    def last(k, place, both):
        qv = qbuf[k]
        o = acc[k] + attend(LAST, 1 - c, qv)
        if both:
            o = o + attend(LAST, c, qv)
        o = o / denom
        asend[k] = o.astype(jnp.bfloat16)
        xx = lax.rem(x + 4 - lax.rem(steps_x // place, 4), 4)
        zz = lax.rem(z + 4 - lax.rem(steps_z // place, 4), 4)

        @pl.when(k < 7)
        def _():
            pltpu.make_async_remote_copy(
                src_ref=asend.at[k],
                dst_ref=abuf.at[mine],
                send_sem=os,
                recv_sem=orr,
                device_id=(y, at(xx, zz, c)),
                device_id_type=MESH,
            ).start()

        return place * 4

    place = lax.fori_loop(0, 4, lambda k, p: last(k, p, False), 1)
    lax.fori_loop(4, 8, lambda k, p: last(k, p, True), place)
    abuf[mine] = asend[7]

    ow_load.wait()
    wait_bytes(abuf.at[pl.ds(0, 7)], orr)
    count = count_ref[y]

    def finish(n, carry):
        rows = pl.ds(pl.multiple_of(n * 128, 128), 128)
        attn = jnp.concatenate([abuf[h, rows, :] for h in range(HEADS)], axis=-1).astype(jnp.float32)
        attn = attn + selfv[rows, :]
        mean = jnp.mean(attn, axis=-1, keepdims=True)
        centered = attn - mean
        var = jnp.mean(centered * centered, axis=-1, keepdims=True)
        normed = centered * lax.rsqrt(var + 1e-05)
        mixed = (normed * projv[rows, 0:D].astype(jnp.float32)).astype(jnp.bfloat16)
        result = xv[rows, :].astype(jnp.float32) + jnp.dot(mixed, owv[...], preferred_element_type=jnp.float32)
        ids = pos * ROWS + n * 128 + lax.broadcasted_iota(jnp.int32, (128, 1), 0)
        out_ref[rows, :] = jnp.where(ids < count, result, 0.0).astype(jnp.bfloat16)
        return carry

    lax.fori_loop(0, ROWS // 128, finish, 0)

    for q in range(NQ):
        wait_bytes(st1[q].at[pl.ds(0, 3)], s1s)
    wait_bytes(qbuf.at[pl.ds(0, 7)], qs)

    wait_bytes(st2.at[pl.ds(0, 3)], s2s)
    for g in range(NS):
        wait_bytes(kvbuf[g].at[:, 0, pl.ds(0, 15)], s3s)
        wait_bytes(kvbuf[g].at[:, 0], xs)
    wait_bytes(abuf.at[pl.ds(0, 7)], os)


def body(cand_x, f1_weight, out_weight, kv_cache, user_slot, hist_len, cand_count):
    bf = jnp.bfloat16
    smem = pl.BlockSpec(memory_space=pltpu.SMEM)
    hbm = pl.BlockSpec(memory_space=pl.ANY)
    dma = pltpu.SemaphoreType.DMA
    out = pl.pallas_call(
        kernel,
        out_shape=jax.ShapeDtypeStruct((ROWS, D), bf),
        in_specs=[smem] * 3 + [hbm] * 4,
        out_specs=pl.BlockSpec(memory_space=pltpu.VMEM),
        scratch_shapes=[
            pltpu.VMEM((ROWS, D), bf),
            pltpu.VMEM((D, 4 * D), bf),
            pltpu.VMEM((D, D), bf),
            pltpu.VMEM((2, HIST, D), bf),
            [pltpu.VMEM((4, 2, R, 2 * HD), bf)] * NQ,
            pltpu.VMEM((4, NQ, 2, 2, R, HD), bf),
            [pltpu.VMEM((4, 2, 2, w, HD), bf) for w in WIDE],
            [pltpu.VMEM((2, 2, 16, w, HD), bf) for w in WIDE],
            pltpu.VMEM((ROWS, 4 * D), bf),
            pltpu.VMEM((8, ROWS, HD), bf),
            pltpu.VMEM((8, ROWS, HD), jnp.float32),
            pltpu.VMEM((8, ROWS, HD), bf),
            pltpu.VMEM((8, ROWS, HD), bf),
            pltpu.VMEM((ROWS, D), jnp.float32),
            dma((4,)),
            dma((4,)),
            dma,
            dma((NQ,)),
            dma,
            dma((NQ,)),
            dma,
            dma((NS,)),
            dma,
            dma((NS,)),
            dma,
            dma,
            dma,
            dma,
            pltpu.SemaphoreType.REGULAR,
        ],
        compiler_params=pltpu.CompilerParams(
            collective_id=0, has_side_effects=True, vmem_limit_bytes=60 * 2**20
        ),
    )(
        user_slot, hist_len, cand_count,
        cand_x.reshape(ROWS, D), f1_weight, out_weight, kv_cache.reshape(HIST, 2 * D),
    )
    return out.reshape(1, ROWS, D)


def solution(mesh):
    placed = (P("group", "pos", None), P(), P(), P("group", "pos", None), P(), P(), P())
    return jax.shard_map(
        body, mesh=mesh, in_specs=placed, out_specs=P("group", "pos", None), check_vma=False
    )
```
